32 devices in a mesh: frames: 2 (over x), chain: 16 (over z, y, core).
Axes of the slice: x: 2, y: 2, z: 4, core: 2. Of those that a mesh axis runs over, the one named last changes fastest.
Arguments:
- species: int32 [8192], P(('frames', 'chain')), parts along dimension 0, may hold values from 0 to 127
- positions: float32 [3, 8192], P(None, ('frames', 'chain')), parts along dimension 1, may hold values from -18 to 18
- block_list: int32 [64, 3], P(('frames', 'chain')), parts along dimension 0, may hold values from -1 to 31, as said below
- embed_table: bfloat16 [128, 512], replicated, may hold values from -6 to 6
- w_query: bfloat16 [2, 512, 512], replicated, may hold values from -0.25 to 0.25
- w_key: bfloat16 [2, 512, 512], replicated, may hold values from -0.25 to 0.25
- w_value: bfloat16 [2, 512, 512], replicated, may hold values from -0.25 to 0.25
- w_out: bfloat16 [2, 512, 512], replicated, may hold values from -0.25 to 0.25
- w_up: bfloat16 [2, 512, 1024], replicated, may hold values from -0.25 to 0.25
- w_down: bfloat16 [2, 1024, 512], replicated, may hold values from -0.1875 to 0.1875
- norm_gains: float32 [2, 2, 512], replicated, may hold values from 0.5 to 1.5
- gammas: float32 [2, 16], replicated, may hold values from 0.005 to 0.1
- out_gain: float32 [512], replicated, may hold values from 0.5 to 1.5
- readout: float32 [512], replicated, may hold values from -0.25 to 0.25
Outputs:
- energy: float32 [2], P('frames'), parts along dimension 0
- forces: float32 [3, 8192], P(None, ('frames', 'chain')), parts along dimension 1
The draws below stay inside these ranges and needn't reach their ends.
There are 2 independent parts, one for each index of `frames`. The reference program is written for one: setup_inputs(seed, part) draws one part's arguments, and reference() takes and returns one part's arrays. A program takes and returns all parts, laid end to end along the dimension named above; an argument that names none is the same for every part. Nothing has to cross between parts.
Inputs may be any that keep to these rules, and one draw needn't show every extreme that they name: `block_list`: row b holds b-1 or -1, then b, then b+1 or -1; -1 marks a neighbouring block outside the cutoff.
All inputs are finite; a program needn't handle non-finite values.
Results may differ from the reference program's by a relative error of at most 0.022.
Values may be sent and summed in bfloat16 or wider, within the bound.
No kernel may reach another device: no remote copies, remote signals or barrier semaphores. Data moves between devices by JAX's collectives and lax.ppermute only.
A program may use at most 128 MiB of HBM per device.

```python
import math
import jax
import jax.numpy as jnp
from jax import lax

D = 512
HEADS = 16
FF = 1024
NSPEC = 128
LAYERS = 2
BLOCKS = 32
ATOMS = 4096


def draw_block_list(key, part):
    ids = jnp.arange(BLOCKS, dtype=jnp.int32)
    key_left, key_right = jax.random.split(jax.random.fold_in(key, 7))
    left = jax.random.randint(key_left, (BLOCKS,), 0, 5) < 3
    right = jax.random.randint(key_right, (BLOCKS,), 0, 5) < 3
    lower = jnp.where(left & (ids > 0), ids - 1, -1)
    upper = jnp.where(right & (ids < BLOCKS - 1), ids + 1, -1)
    return jnp.stack([lower, ids, upper], axis=1).astype(jnp.int32)


def touch_ends(array, own_key, low, largest):
    longest = array.shape.index(max(array.shape))
    spots = []
    for shift in (0, 1):
        where = [jax.random.randint(jax.random.fold_in(own_key, axis), (), 0, length) for axis, length in enumerate(array.shape)]
        where[longest] = (where[longest] + shift) % array.shape[longest]
        spots.append(tuple(where))
    return array.at[spots[0]].set(low).at[spots[1]].set(largest)


def shard_levels(key, shape, shards, smallest, largest):
    def one(axis_at, blocks):
        draws = jax.random.uniform(jax.random.fold_in(jax.random.fold_in(key, 6), axis_at), (blocks,), jnp.float32, smallest / len(shards), largest / len(shards))
        return jnp.repeat(jnp.exp(draws), shape[axis_at] // blocks).reshape((-1,) + (1,) * (len(shape) - axis_at - 1))

    level = one(*shards[0])
    for cut in shards[1:]:
        level = level * one(*cut)
    return level


def gaussian(own_key, extent, scale, bound, cuts=(), held_as=jnp.bfloat16):
    values = scale * jax.random.normal(own_key, extent, jnp.float32)
    if cuts:
        values = values * shard_levels(own_key, extent, cuts, -0.22, 0.18)
    return jnp.clip(values, -bound, bound).astype(held_as)


def setup_inputs(seed: int = 0, part: int = 0) -> dict:
    key_list = jax.random.split(jax.random.key(seed), 15)
    part_keys = jax.random.split(jax.random.fold_in(key_list[14], part), 15)
    species = touch_ends(jax.random.randint(part_keys[0], (ATOMS,), 0, NSPEC), jax.random.fold_in(part_keys[0], 1), 0, NSPEC - 1).astype(jnp.int32)
    positions = gaussian(part_keys[1], (3, ATOMS), 3.0, 18.0, ((1, 16),), jnp.float32)
    block_list = draw_block_list(jax.random.fold_in(jax.random.fold_in(key_list[14], part), 71), part)
    embed_table = gaussian(key_list[3], (NSPEC, D), 1.0, 6.0)
    w_query = gaussian(key_list[4], (LAYERS, D, D), D ** -0.5, 0.25)
    w_key = gaussian(key_list[5], (LAYERS, D, D), D ** -0.5, 0.25)
    w_value = gaussian(key_list[6], (LAYERS, D, D), D ** -0.5, 0.25)
    w_out = gaussian(key_list[7], (LAYERS, D, D), D ** -0.5, 0.25)
    w_up = gaussian(key_list[8], (LAYERS, D, FF), D ** -0.5, 0.25)
    w_down = gaussian(key_list[9], (LAYERS, FF, D), FF ** -0.5, 0.1875)
    norm_gains = jnp.clip(1.0 + 0.1 * jax.random.normal(key_list[10], (LAYERS, 2, D), jnp.float32), 0.5, 1.5)
    gammas = jnp.clip(jnp.exp(jax.random.uniform(key_list[11], (LAYERS, HEADS), jnp.float32, math.log(0.005), math.log(0.1))), 0.005, 0.1)
    out_gain = jnp.clip(1.0 + 0.1 * jax.random.normal(key_list[12], (D,), jnp.float32), 0.5, 1.5)
    readout = gaussian(key_list[13], (D,), D ** -0.5, 0.25, (), jnp.float32)
    return {"species": species, "positions": positions, "block_list": block_list, "embed_table": embed_table, "w_query": w_query, "w_key": w_key, "w_value": w_value, "w_out": w_out, "w_up": w_up, "w_down": w_down, "norm_gains": norm_gains, "gammas": gammas, "out_gain": out_gain, "readout": readout}


def rms(x, gain):
    return x * lax.rsqrt(lax.optimization_barrier(jnp.mean(x * x, axis=-1, keepdims=True)) + 1e-06) * gain

def windows(ext, nblk):
    blocks = ext.reshape(nblk + 2, 128, ext.shape[-1])
    return jnp.concatenate([blocks[:-2], blocks[1:-1], blocks[2:]], axis=1)

def attend(query, key_ext, value_ext, coord, coord_ext, valid, gamma, heads):
    atoms, width = query.shape
    nblk = atoms // 128
    hdim = width // heads
    key_win = windows(key_ext, nblk).astype(jnp.bfloat16).reshape(nblk, 384, heads, hdim)
    value_win = windows(value_ext, nblk).astype(jnp.bfloat16).reshape(nblk, 384, heads, hdim)
    query_blk = query.reshape(nblk, 128, heads, hdim)
    scores = jnp.einsum('bqhd,bkhd->bhqk', query_blk.astype(jnp.float32), key_win.astype(jnp.float32), precision=lax.Precision.HIGHEST) * hdim ** (-0.5)
    coord_blk = coord_ext.reshape(3, nblk + 2, 128)
    coord_win = jnp.concatenate([coord_blk[:, :-2], coord_blk[:, 1:-1], coord_blk[:, 2:]], axis=2)
    coord_q = coord.reshape(3, nblk, 128)
    dist_sq = lax.optimization_barrier(jnp.sum((coord_q[:, :, :, None] - coord_win[:, :, None, :]) ** 2, axis=0))
    scores = scores - gamma[None, :, None, None] * dist_sq[:, None]
    keymask = jnp.repeat(valid, 128, axis=1)
    scores = jnp.where(keymask[:, None, None, :], scores, -1e+30)
    peak = lax.stop_gradient(lax.optimization_barrier(jnp.max(scores, axis=-1, keepdims=True)))
    expo = jnp.exp(scores - peak)
    probs = (expo / lax.optimization_barrier(jnp.sum(expo, axis=-1, keepdims=True))).astype(jnp.bfloat16)
    mixed = jnp.einsum('bhqk,bkhd->bqhd', probs.astype(jnp.float32), value_win.astype(jnp.float32), precision=lax.Precision.HIGHEST)
    return mixed.reshape(atoms, width).astype(jnp.bfloat16)

def energy_of(positions, species, valid, embed_table, w_query, w_key, w_value, w_out, w_up, w_down, norm_gains, gammas, out_gain, readout):
    heads = gammas.shape[1]
    onehot = jax.nn.one_hot(species, embed_table.shape[0], dtype=jnp.bfloat16)
    state = jnp.dot(onehot, embed_table, preferred_element_type=jnp.float32)
    for layer in range(w_query.shape[0]):
        normed = rms(state, norm_gains[layer, 0]).astype(jnp.bfloat16)
        query = jnp.dot(normed, w_query[layer], preferred_element_type=jnp.float32).astype(jnp.bfloat16)
        keys = jnp.dot(normed, w_key[layer], preferred_element_type=jnp.float32).astype(jnp.bfloat16)
        values = jnp.dot(normed, w_value[layer], preferred_element_type=jnp.float32).astype(jnp.bfloat16)
        key_ext = jnp.pad(keys.astype(jnp.float32), ((128, 128), (0, 0)))
        value_ext = jnp.pad(values.astype(jnp.float32), ((128, 128), (0, 0)))
        coord_ext = jnp.pad(positions, ((0, 0), (128, 128)))
        att = attend(query, key_ext, value_ext, positions, coord_ext, valid, gammas[layer], heads)
        state = state + jnp.dot(att, w_out[layer], preferred_element_type=jnp.float32)
        inner = rms(state, norm_gains[layer, 1]).astype(jnp.bfloat16)
        hidden = jax.nn.gelu(jnp.dot(inner, w_up[layer], preferred_element_type=jnp.float32)).astype(jnp.bfloat16)
        state = state + jnp.dot(hidden, w_down[layer], preferred_element_type=jnp.float32)
    per_atom = jnp.dot(rms(state, out_gain), readout, precision=lax.Precision.HIGHEST)
    return jnp.sum(per_atom)

def reference(species, positions, block_list, embed_table, w_query, w_key, w_value, w_out, w_up, w_down, norm_gains, gammas, out_gain, readout):
    nblk = block_list.shape[0]
    ids = jnp.arange(nblk, dtype=jnp.int32)
    expect = ids[:, None] - 1 + jnp.arange(3, dtype=jnp.int32)[None, :]
    valid = (block_list == expect) & (block_list >= 0)

    def total(coords):
        return energy_of(coords, species, valid, embed_table, w_query, w_key, w_value, w_out, w_up, w_down, norm_gains, gammas, out_gain, readout)
    value, pullback = jax.vjp(total, positions)
    grad, = pullback(jnp.ones((), value.dtype))
    return (value.reshape(1), -grad)
```

```python
import functools
import math

import jax
import jax.numpy as jnp
from jax import lax
from jax.experimental import pallas as pl
from jax.experimental.pallas import tpu as pltpu
from jax.sharding import PartitionSpec as P

BLK = 128
LANES = 128
EPS = 1e-06
LOG2E = math.log2(math.e)
LN2 = math.log(2.0)
FAR = 1e30
F32 = jnp.float32
BF16 = jnp.bfloat16
C0 = math.sqrt(2.0 / math.pi)
C1 = 0.044715


def mm(a, b):
    return jnp.dot(a, b, preferred_element_type=F32)


def mm_nt(a, b):
    return lax.dot_general(a, b, (((1,), (1,)), ((), ())), preferred_element_type=F32)


def mm_tn(a, b):
    return lax.dot_general(a, b, (((0,), (0,)), ((), ())), preferred_element_type=F32)


def inv_rms(x):
    return lax.rsqrt(jnp.mean(x * x, axis=-1, keepdims=True) + EPS)


def rms_back(x, gain, cot):
    r = inv_rms(x)
    t = cot * gain
    return r * (t - x * (r * r * jnp.mean(x * t, axis=-1, keepdims=True)))


def gelu_both(x):
    t = jnp.tanh(C0 * (x + C1 * x * x * x))
    half = 0.5 * (1.0 + t)
    return x * half, half + 0.5 * x * (1.0 - t * t) * (C0 + 3.0 * C0 * C1 * x * x)


def head_masks(rows, heads_per_group, hdim):
    lane = lax.broadcasted_iota(jnp.int32, (rows, LANES), 1) // hdim
    return [(lane == h).astype(F32).astype(BF16) for h in range(heads_per_group)]


def arrange(par, own, from_a, from_b):
    before = jnp.where(par == 0, from_b, from_a)
    after = jnp.where(par == 0, from_a, from_b)
    return before, own, after


def distances(ext, ext_t, first, d2_ref, count):
    for i in range(count):
        q = ext_t[(first + i) * BLK : (first + i + 1) * BLK]
        for s in range(3):
            k0 = (first + i - 1 + s) * BLK
            tot = None
            for c in range(3):
                diff = q[:, c : c + 1] - ext[c : c + 1, k0 : k0 + BLK]
                tot = diff * diff if tot is None else tot + diff * diff
            d2_ref[i, :, s * BLK : (s + 1) * BLK] = jnp.where(q[:, 4 + s : 5 + s] > 0.5, tot, FAR)


def attend(q_ref, k_ref, v_ref, o_ref, rl_ref, e_ref, d2_ref, d2_first, gam_ref, layer, heads, hdim, count):
    per = LANES // hdim
    groups = heads // per
    mask = head_masks(BLK, per, hdim)
    mask3 = head_masks(3 * BLK, per, hdim)
    for i in range(count):
        for g in range(groups):
            cols = slice(g * LANES, (g + 1) * LANES)
            q = q_ref[i * BLK : (i + 1) * BLK, cols]
            k = k_ref[i * BLK : (i + 3) * BLK, cols]
            v = v_ref[i * BLK : (i + 3) * BLK, cols]
            qs = jnp.concatenate([q * m for m in mask], axis=0)
            scores = mm_nt(qs, k)
            d2 = d2_ref[d2_first + i]
            parts = []
            for h in range(per):
                gam = gam_ref[layer, g * per + h] * LOG2E
                s = scores[h * BLK : (h + 1) * BLK] - gam * d2
                e = jnp.exp2(s - jnp.max(s, axis=1, keepdims=True)).astype(BF16)
                e_ref[i, g * per + h] = e
                parts.append(e)
            vs = jnp.concatenate(
                [jnp.concatenate([v * m for m in mask3], axis=0), jnp.concatenate(mask3, axis=0)], axis=1
            )
            out = mm(jnp.concatenate(parts, axis=1), vs)
            rl = 1.0 / out[:, LANES:]
            rl_ref[i * BLK : (i + 1) * BLK, cols] = rl
            o_ref[i * BLK : (i + 1) * BLK, cols] = (out[:, :LANES] * rl).astype(BF16)


def delta_of(prod, per, hdim):
    lane = lax.broadcasted_iota(jnp.int32, prod.shape, 1) // hdim
    return [jnp.sum(jnp.where(lane == h, prod, 0.0), axis=1, keepdims=True) for h in range(per)]


def fold(grad, ext, ext_t, qb, kb):
    cols, rows = [], []
    for c in range(3):
        diff = ext_t[qb * BLK : (qb + 1) * BLK, c : c + 1] - ext[c : c + 1, kb * BLK : (kb + 1) * BLK]
        t = grad * diff
        cols.append(2.0 * jnp.sum(t, axis=1, keepdims=True))
        rows.append(-2.0 * jnp.sum(t, axis=0, keepdims=True))
    return cols, rows


def columns_to_rows(cols):
    lane = lax.broadcasted_iota(jnp.int32, (BLK, LANES), 1)
    wide = jnp.zeros((BLK, LANES), F32)
    for c in range(3):
        wide = jnp.where(lane == c, cols[c], wide)
    return wide.T[:8]


def three_rows(rows):
    sub = lax.broadcasted_iota(jnp.int32, (8, LANES), 0)
    out = jnp.zeros((8, LANES), F32)
    for c in range(3):
        out = jnp.where(sub == c, rows[c], out)
    return out


def first_kernel(
    nb, heads, hdim,
    par_ref, gam_ref, own_ref, ra_ref, rb_ref, embed_ref, gains_ref, outg_ref, ro_ref,
    wq_h, wk_h, wv_h, wo_h, wu_h, wd_h,
    e_out, paya_ref, payb_ref, part_ref, halo_ref, g1_ref,
    s_o, s_rl, s_v, s_x1, s_gd, s_e, s_el, s_er,
    wq, wk, wv, wo, wu, wd, wsem, osem,
    d2_ref, x0_ref, q_ref, k_ref, v_ref, o_ref, rl_ref, e_ref, x1_ref, gd_ref, st_ref,
    q1_ref, k1_ref, v1_ref, o1_ref, rl1_ref, e1_ref, dq_ref, dk_ref, dv_ref,
):
    layers = 2
    qb = nb + 2
    kb = nb + 4
    mid = slice(BLK, (nb + 1) * BLK)
    copies = {}
    for layer in range(layers):
        for n, (src, dst) in enumerate(((wq_h, wq), (wk_h, wk), (wv_h, wv), (wo_h, wo), (wu_h, wu), (wd_h, wd))):
            copies[n, layer] = pltpu.make_async_copy(src.at[layer], dst.at[layer], wsem.at[n, layer])
            copies[n, layer].start()

    par = par_ref[0]
    before, own, after = arrange(par, own_ref[...], ra_ref[...], rb_ref[...])
    ext = jnp.concatenate([before, own, after], axis=1)
    ext_t = ext.T
    distances(ext, ext_t, 1, d2_ref, qb)

    embed = embed_ref[...].astype(F32)
    normed = (embed * inv_rms(embed) * gains_ref[0:1]).astype(BF16)
    scale = hdim ** (-0.5)
    spec = ext_t[:, 3:4].astype(jnp.int32)
    nspec = embed_ref.shape[0]
    onehot = (spec == lax.broadcasted_iota(jnp.int32, (kb * BLK, nspec), 1)).astype(F32).astype(BF16)
    onehot_q = onehot[BLK : (qb + 1) * BLK]
    x0_ref[...] = mm(onehot_q, embed_ref[...])
    copies[0, 0].wait()
    q_ref[...] = mm(onehot_q, (mm(normed, wq[0]) * (scale * LOG2E)).astype(BF16)).astype(BF16)
    copies[1, 0].wait()
    k_ref[...] = mm(onehot, mm(normed, wk[0]).astype(BF16)).astype(BF16)
    copies[2, 0].wait()
    v_ref[...] = mm(onehot, mm(normed, wv[0]).astype(BF16)).astype(BF16)
    attend(q_ref, k_ref, v_ref, o_ref, rl_ref, e_ref, d2_ref, 0, gam_ref, 0, heads, hdim, qb)
    outs = [
        pltpu.make_async_copy(o_ref, s_o, osem.at[0]),
        pltpu.make_async_copy(rl_ref, s_rl, osem.at[1]),
        pltpu.make_async_copy(v_ref.at[pl.ds(BLK, qb * BLK)], s_v, osem.at[2]),
        pltpu.make_async_copy(e_ref.at[pl.ds(1, nb)], s_e, osem.at[3]),
        pltpu.make_async_copy(e_ref.at[0, :, :, pl.ds(2 * BLK, BLK)], s_el, osem.at[4]),
        pltpu.make_async_copy(e_ref.at[qb - 1, :, :, pl.ds(0, BLK)], s_er, osem.at[5]),
    ]
    for c in outs:
        c.start()
    copies[3, 0].wait()
    copies[4, 0].wait()
    copies[5, 0].wait()

    def feed(layer, x1, keep):
        inner = (x1 * inv_rms(x1) * gains_ref[2 * layer + 1 : 2 * layer + 2]).astype(BF16)
        act, slope = gelu_both(mm(inner, wu[layer]))
        keep(slope.astype(BF16))
        return x1 + mm(act.astype(BF16), wd[layer])

    step = 2 * BLK
    for r in range(0, qb * BLK, step):
        rows = slice(r, r + step)
        x1 = x0_ref[rows] + mm(o_ref[rows], wo[0])
        x1_ref[rows] = x1
        st_ref[rows] = feed(0, x1, lambda slope: gd_ref.__setitem__(rows, slope))
    outs += [
        pltpu.make_async_copy(x1_ref, s_x1, osem.at[6]),
        pltpu.make_async_copy(gd_ref, s_gd, osem.at[7]),
    ]
    for c in outs[6:]:
        c.start()

    for n in range(6):
        copies[n, 1].wait()
    gain = gains_ref[2:3]
    st = st_ref[...]
    normed = (st * inv_rms(st) * gain).astype(BF16)
    q1_ref[...] = (mm(normed[mid], wq[1]) * (scale * LOG2E)).astype(BF16)
    k1_ref[...] = mm(normed, wk[1]).astype(BF16)
    v1_ref[...] = mm(normed, wv[1]).astype(BF16)
    attend(q1_ref, k1_ref, v1_ref, o1_ref, rl1_ref, e1_ref, d2_ref, 1, gam_ref, 1, heads, hdim, nb)
    x1 = st_ref[mid] + mm(o1_ref[...], wo[1])
    slopes = []
    x2 = feed(1, x1, slopes.append)
    (slope,) = slopes

    w = outg_ref[...] * ro_ref[...]
    r = inv_rms(x2)
    along = jnp.sum(x2 * w, axis=1, keepdims=True)
    e_out[...] = jnp.broadcast_to(jnp.sum(along * r), e_out.shape)
    width = x2.shape[1]
    grad = r * (w - x2 * (r * r * along * (1.0 / width)))

    du = mm_nt(grad.astype(BF16), wd[1]).astype(BF16).astype(F32)
    dinner = mm_nt((du * slope.astype(F32)).astype(BF16), wu[1]).astype(BF16).astype(F32)
    grad = grad + rms_back(x1, gains_ref[3:4], dinner)
    datt = mm_nt(grad.astype(BF16), wo[1]).astype(BF16).astype(F32)

    per = LANES // hdim
    groups = heads // per
    mask = head_masks(BLK, per, hdim)
    mask3 = head_masks(3 * BLK, per, hdim)
    dk_ref[...] = jnp.zeros_like(dk_ref)
    dv_ref[...] = jnp.zeros_like(dv_ref)
    for i in range(nb):
        rows = slice(i * BLK, (i + 1) * BLK)
        win = slice(i * BLK, (i + 3) * BLK)
        pair = jnp.zeros((BLK, 3 * BLK), F32)
        for g in range(groups):
            cols = slice(g * LANES, (g + 1) * LANES)
            d_o = datt[rows, cols] * rl1_ref[rows, cols]
            delta = delta_of(d_o * o1_ref[rows, cols].astype(F32), per, hdim)
            d_o = d_o.astype(BF16)
            dos = jnp.concatenate([d_o * m for m in mask], axis=0)
            k = k1_ref[win, cols]
            q = q1_ref[rows, cols]
            qs = jnp.concatenate([q * m for m in mask], axis=0)
            dp = mm_nt(dos, v1_ref[win, cols])
            parts, es = [], []
            for h in range(per):
                e = e1_ref[i, g * per + h]
                ds = e.astype(F32) * (dp[h * BLK : (h + 1) * BLK] - delta[h])
                pair = pair + gam_ref[1, g * per + h] * ds
                parts.append(ds.astype(BF16))
                es.append(e)
            ks = jnp.concatenate([k * m for m in mask3], axis=0)
            dq_ref[rows, cols] = (mm(jnp.concatenate(parts, axis=1), ks) * scale).astype(BF16)
            dk_ref[win, cols] += mm_tn(jnp.concatenate(parts, axis=0), qs)
            dv_ref[win, cols] += mm_tn(jnp.concatenate(es, axis=0), dos)
        g1_ref[i] = pair
    dk = (dk_ref[...] * LN2).astype(BF16)
    dv = dv_ref[...].astype(BF16)
    dnorm = mm_nt(dk, wk[1]) + mm_nt(dv, wv[1])
    dq = mm_nt(dq_ref[...], wq[1])
    zeros = jnp.zeros((BLK, width), F32)
    dnorm = dnorm + jnp.concatenate([zeros, dq, zeros], axis=0)
    back = rms_back(st_ref[...], gain, dnorm.astype(BF16).astype(F32))
    part = grad + back[mid]
    part_ref[...] = part
    halo_ref[:BLK] = back[:BLK]
    halo_ref[BLK:] = back[(qb - 1) * BLK :]

    _, rows_low = fold(g1_ref[0, :, :BLK], ext, ext_t, 2, 1)
    _, rows_high = fold(g1_ref[nb - 1, :, 2 * BLK :], ext, ext_t, nb + 1, nb + 2)
    pad = jnp.zeros((8, width - LANES), F32)

    def payload(ref, halo, edge, rows):
        ref[:BLK] = halo.astype(BF16)
        ref[BLK : 2 * BLK] = edge.astype(BF16)
        tail = jnp.concatenate([three_rows(rows), pad], axis=1)
        ref[2 * BLK :] = jnp.concatenate([tail, jnp.zeros_like(tail)], axis=0).astype(BF16)

    def low(ref):
        payload(ref, back[:BLK], part[:BLK], rows_low)

    def high(ref):
        payload(ref, back[(qb - 1) * BLK :], part[(nb - 1) * BLK :], rows_high)

    @pl.when(par == 0)
    def _():
        high(paya_ref)
        low(payb_ref)

    @pl.when(par != 0)
    def _():
        low(paya_ref)
        high(payb_ref)

    for c in outs:
        c.wait()


def second_kernel(
    nb, heads, hdim,
    par_ref, gam_ref, own_ref, ra_ref, rb_ref, gains_ref, paya_ref, payb_ref, part_ref, halo_ref, g1_ref,
    s_o, s_rl, s_v, s_x1, s_gd, s_e, s_el, s_er, wo_h, wu_h, wd_h,
    f_ref,
    o_ref, rl_ref, v_ref, x1_ref, gd_ref, e_ref, el_ref, er_ref, wo, wu, wd, sem,
    datt_ref,
):
    qb = nb + 2
    pairs = (
        (wd_h.at[0], wd), (s_gd, gd_ref), (wu_h.at[0], wu), (s_x1, x1_ref), (wo_h.at[0], wo),
        (s_rl, rl_ref), (s_o, o_ref), (s_v, v_ref), (s_e, e_ref), (s_el, el_ref), (s_er, er_ref),
    )
    copies = [pltpu.make_async_copy(src, dst, sem.at[n]) for n, (src, dst) in enumerate(pairs)]
    for c in copies:
        c.start()
    par = par_ref[0]
    before, own, after = arrange(par, own_ref[...], ra_ref[...], rb_ref[...])
    ext = jnp.concatenate([before, own, after], axis=1)
    ext_t = ext.T
    from_low, _, from_high = arrange(par, None, paya_ref[...], payb_ref[...])
    from_low = from_low.astype(F32)
    from_high = from_high.astype(F32)
    part = part_ref[...]
    pieces = [halo_ref[:BLK] + from_low[BLK : 2 * BLK]]
    own_parts = [part[i * BLK : (i + 1) * BLK] for i in range(nb)]
    own_parts[0] = own_parts[0] + from_low[:BLK]
    own_parts[-1] = own_parts[-1] + from_high[:BLK]
    pieces += own_parts
    pieces.append(halo_ref[BLK:] + from_high[BLK : 2 * BLK])
    grad = jnp.concatenate(pieces, axis=0)
    copies[0].wait()
    du = mm_nt(grad.astype(BF16), wd[...]).astype(BF16).astype(F32)
    copies[1].wait()
    copies[2].wait()
    dinner = mm_nt((du * gd_ref[...].astype(F32)).astype(BF16), wu[...]).astype(BF16).astype(F32)
    copies[3].wait()
    grad = grad + rms_back(x1_ref[...], gains_ref[1:2], dinner)
    copies[4].wait()
    datt_ref[...] = mm_nt(grad.astype(BF16), wo[...]).astype(BF16).astype(F32)
    for c in copies[5:]:
        c.wait()

    per = LANES // hdim
    groups = heads // per
    mask = head_masks(BLK, per, hdim)

    def pair_of(rows, keys, e_of, total):
        for g in range(groups):
            cols = slice(g * LANES, (g + 1) * LANES)
            d_o = datt_ref[rows, cols] * rl_ref[rows, cols]
            delta = delta_of(d_o * o_ref[rows, cols].astype(F32), per, hdim)
            d_o = d_o.astype(BF16)
            dos = jnp.concatenate([d_o * m for m in mask], axis=0)
            dp = mm_nt(dos, v_ref[keys, cols])
            for h in range(per):
                ds = e_of(g * per + h).astype(F32) * (dp[h * BLK : (h + 1) * BLK] - delta[h])
                total = total + gam_ref[0, g * per + h] * ds
        return total

    forces = [jnp.zeros((8, LANES), F32) for _ in range(nb)]
    forces[0] = forces[0] + from_low[2 * BLK : 2 * BLK + 8, :LANES]
    forces[-1] = forces[-1] + from_high[2 * BLK : 2 * BLK + 8, :LANES]
    for i in range(nb):
        total = pair_of(
            slice((i + 1) * BLK, (i + 2) * BLK), slice(i * BLK, (i + 3) * BLK), lambda h: e_ref[i, h], g1_ref[i]
        )
        sums = None
        for s in range(3):
            cols, rows = fold(total[:, s * BLK : (s + 1) * BLK], ext, ext_t, i + 2, i + 1 + s)
            sums = cols if sums is None else [a + b for a, b in zip(sums, cols)]
            j = i - 1 + s
            if 0 <= j < nb:
                forces[j] = forces[j] + three_rows(rows)
        forces[i] = forces[i] + columns_to_rows(sums)
    zero = jnp.zeros((BLK, BLK), F32)
    total = pair_of(slice(0, BLK), slice(BLK, 2 * BLK), lambda h: el_ref[h], zero)
    _, rows = fold(total, ext, ext_t, 1, 2)
    forces[0] = forces[0] + three_rows(rows)
    total = pair_of(slice((qb - 1) * BLK, qb * BLK), slice((qb - 2) * BLK, (qb - 1) * BLK), lambda h: er_ref[h], zero)
    _, rows = fold(total, ext, ext_t, nb + 2, nb + 1)
    forces[-1] = forces[-1] + three_rows(rows)
    f_ref[...] = jnp.concatenate(forces, axis=1)[:3]


def swap_a(x):
    n = lax.axis_size("chain")
    return lax.ppermute(x, "chain", [(i, i ^ 1) for i in range(n)])


def swap_b(x):
    n = lax.axis_size("chain")
    return lax.ppermute(x, "chain", [(i, ((i + 1) ^ 1) - 1) for i in range(1, n - 1)])


def total_of(x):
    n = lax.axis_size("chain")
    if n & (n - 1):
        return lax.psum(x, "chain")
    step = 1
    while step < n:
        x = x + lax.ppermute(x, "chain", [(i, i ^ step) for i in range(n)])
        step *= 2
    return x


def local(
    species, positions, block_list, embed, w_query, w_key, w_value, w_out, w_up, w_down, norm_gains, gammas, out_gain, readout
):
    atoms = species.shape[0]
    nb = atoms // BLK
    width = embed.shape[1]
    layers, heads = gammas.shape
    hdim = width // heads
    ff = w_up.shape[2]
    qb, kb = nb + 2, nb + 4
    assert nb >= 2 and layers == 2 and LANES % hdim == 0
    me = lax.axis_index("chain")
    par = (me % 2).astype(jnp.int32).reshape(1)
    expect = (me * nb + jnp.arange(nb, dtype=jnp.int32))[:, None] - 1 + jnp.arange(3, dtype=jnp.int32)[None, :]
    valid = ((block_list == expect) & (block_list >= 0)).astype(F32)
    own = jnp.concatenate(
        [positions, species.astype(F32)[None], jnp.repeat(valid.T, BLK, axis=1), jnp.zeros((1, atoms), F32)], axis=0
    )
    edge = 2 * BLK
    if atoms == edge:
        send_a = send_b = own
    else:
        first, last = own[:, :edge], own[:, -edge:]
        send_a = jnp.where(par[0] == 0, last, first)
        send_b = jnp.where(par[0] == 0, first, last)
    near_a, near_b = swap_a(send_a), swap_b(send_b)
    gains = norm_gains.reshape(2 * layers, width)
    smem = pl.BlockSpec(memory_space=pltpu.SMEM)
    vmem = pl.BlockSpec(memory_space=pltpu.VMEM)
    hbm = pl.BlockSpec(memory_space=pltpu.HBM)

    def out(*shape, dtype=F32):
        return jax.ShapeDtypeStruct(shape, dtype)

    pay = out(2 * BLK + 16, width, dtype=BF16)
    saved = [
        out(qb * BLK, width, dtype=BF16),
        out(qb * BLK, width),
        out(qb * BLK, width, dtype=BF16),
        out(qb * BLK, width),
        out(qb * BLK, ff, dtype=BF16),
        out(nb, heads, BLK, 3 * BLK, dtype=BF16),
        out(heads, BLK, BLK, dtype=BF16),
        out(heads, BLK, BLK, dtype=BF16),
    ]
    vm = pltpu.VMEM
    first = pl.pallas_call(
        functools.partial(first_kernel, nb, heads, hdim),
        out_shape=[
            out(8, LANES), pay, pay, out(nb * BLK, width), out(2 * BLK, width), out(nb, BLK, 3 * BLK), *saved,
        ],
        in_specs=[smem, smem] + [vmem] * 7 + [hbm] * 6,
        out_specs=[vmem] * 6 + [hbm] * 8,
        scratch_shapes=[
            vm((layers, width, width), BF16), vm((layers, width, width), BF16), vm((layers, width, width), BF16),
            vm((layers, width, width), BF16), vm((layers, width, ff), BF16), vm((layers, ff, width), BF16),
            pltpu.SemaphoreType.DMA((6, layers)), pltpu.SemaphoreType.DMA((8,)),
            vm((qb, BLK, 3 * BLK), F32), vm((qb * BLK, width), F32), vm((qb * BLK, width), BF16),
            vm((kb * BLK, width), BF16), vm((kb * BLK, width), BF16), vm((qb * BLK, width), BF16),
            vm((qb * BLK, width), F32), vm((qb, heads, BLK, 3 * BLK), BF16), vm((qb * BLK, width), F32),
            vm((qb * BLK, ff), BF16), vm((qb * BLK, width), F32),
            vm((nb * BLK, width), BF16), vm((qb * BLK, width), BF16), vm((qb * BLK, width), BF16),
            vm((nb * BLK, width), BF16), vm((nb * BLK, width), F32), vm((nb, heads, BLK, 3 * BLK), BF16),
            vm((nb * BLK, width), BF16), vm((qb * BLK, width), F32), vm((qb * BLK, width), F32),
        ],
        compiler_params=pltpu.CompilerParams(vmem_limit_bytes=62 * 1024 * 1024),
    )(
        par, gammas, own, near_a, near_b, embed, gains, out_gain.reshape(1, width), readout.reshape(1, width),
        w_query, w_key, w_value, w_out, w_up, w_down,
    )
    e_part, pay_a, pay_b, part, halo, g1 = first[:6]
    got_a, got_b = swap_a(pay_a), swap_b(pay_b)
    energy = total_of(e_part[:1, :1]).reshape(1)
    forces = pl.pallas_call(
        functools.partial(second_kernel, nb, heads, hdim),
        out_shape=out(3, atoms),
        in_specs=[smem, smem] + [vmem] * 9 + [hbm] * 11,
        out_specs=vmem,
        scratch_shapes=[
            vm((qb * BLK, width), BF16), vm((qb * BLK, width), F32), vm((qb * BLK, width), BF16),
            vm((qb * BLK, width), F32), vm((qb * BLK, ff), BF16), vm((nb, heads, BLK, 3 * BLK), BF16),
            vm((heads, BLK, BLK), BF16), vm((heads, BLK, BLK), BF16),
            vm((width, width), BF16), vm((width, ff), BF16), vm((ff, width), BF16),
            pltpu.SemaphoreType.DMA((11,)),
            vm((qb * BLK, width), F32),
        ],
        compiler_params=pltpu.CompilerParams(vmem_limit_bytes=62 * 1024 * 1024),
    )(par, gammas, own, near_a, near_b, gains, got_a, got_b, part, halo, g1, *first[6:], w_out, w_up, w_down)
    return energy, forces


def solution(mesh):
    sharded = ("frames", "chain")
    return jax.shard_map(
        local,
        mesh=mesh,
        in_specs=(P(sharded), P(None, sharded), P(sharded, None)) + (P(),) * 11,
        out_specs=(P("frames"), P(None, sharded)),
        check_vma=False,
    )
```

```python
import functools
import math

import jax
import jax.numpy as jnp
from jax import lax
from jax.experimental import pallas as pl
from jax.experimental.pallas import tpu as pltpu
from jax.sharding import PartitionSpec as P

BLK = 128
LANES = 128
EPS = 1e-06
LOG2E = math.log2(math.e)
LN2 = math.log(2.0)
FAR = 1e30
F32 = jnp.float32
BF16 = jnp.bfloat16
C0 = math.sqrt(2.0 / math.pi)
C1 = 0.044715


def mm(a, b):
    return jnp.dot(a, b, preferred_element_type=F32)


def mm_nt(a, b):
    return lax.dot_general(a, b, (((1,), (1,)), ((), ())), preferred_element_type=F32)


def mm_tn(a, b):
    return lax.dot_general(a, b, (((0,), (0,)), ((), ())), preferred_element_type=F32)


def inv_rms(x):
    return lax.rsqrt(jnp.mean(x * x, axis=-1, keepdims=True) + EPS)


def rms_back(x, gain, cot):
    r = inv_rms(x)
    t = cot * gain
    return r * (t - x * (r * r * jnp.mean(x * t, axis=-1, keepdims=True)))


def gelu_both(x):
    t = jnp.tanh(C0 * (x + C1 * x * x * x))
    half = 0.5 * (1.0 + t)
    return x * half, half + 0.5 * x * (1.0 - t * t) * (C0 + 3.0 * C0 * C1 * x * x)


def head_masks(rows, heads_per_group, hdim):
    lane = lax.broadcasted_iota(jnp.int32, (rows, LANES), 1) // hdim
    return [(lane == h).astype(F32).astype(BF16) for h in range(heads_per_group)]


def arrange(par, own, from_a, from_b):
    before = jnp.where(par == 0, from_b, from_a)
    after = jnp.where(par == 0, from_a, from_b)
    return before, own, after


def distances(ext, ext_t, first, d2_ref, count):
    for i in range(count):
        q = ext_t[(first + i) * BLK : (first + i + 1) * BLK]
        for s in range(3):
            k0 = (first + i - 1 + s) * BLK
            tot = None
            for c in range(3):
                diff = q[:, c : c + 1] - ext[c : c + 1, k0 : k0 + BLK]
                tot = diff * diff if tot is None else tot + diff * diff
            d2_ref[i, :, s * BLK : (s + 1) * BLK] = jnp.where(q[:, 4 + s : 5 + s] > 0.5, tot, FAR)


def stacked(x, masks):
    return jnp.concatenate([x * m for m in masks], axis=0)


def beside(x, y):
    zero = jnp.zeros_like(x)
    return jnp.concatenate([jnp.concatenate([x, zero], axis=1), jnp.concatenate([zero, y], axis=1)], axis=0)


def pair_products(a, b, masks, masks2, per):
    shared = mm_nt(stacked(a, masks2), b[BLK : 3 * BLK])
    both = jnp.concatenate([a[:BLK], a[BLK:]], axis=1)
    both = jnp.concatenate([both * jnp.concatenate([m, m], axis=1) for m in masks], axis=0)
    outer = mm_nt(both, beside(b[:BLK], b[3 * BLK :]))
    got = []
    for t in range(2):
        got.append([
            (outer[h * BLK : (h + 1) * BLK, t * BLK : (t + 1) * BLK], shared[(2 * h + t) * BLK : (2 * h + t + 1) * BLK])
            for h in range(per)
        ])
    return got


def window_parts(t):
    return (slice(0, BLK), slice(BLK, 3 * BLK)) if t == 0 else (slice(2 * BLK, 3 * BLK), slice(0, 2 * BLK))


def attend(q_ref, k_ref, v_ref, o_ref, rl_ref, e_ref, d2_ref, d2_first, gam_ref, layer, heads, hdim, count):
    per = LANES // hdim
    groups = heads // per
    masks = head_masks(BLK, per, hdim)
    masks2 = head_masks(2 * BLK, per, hdim)
    masks3 = head_masks(3 * BLK, per, hdim)
    ones = jnp.concatenate(masks3, axis=0)
    for i in range(0, count, 2):
        for g in range(groups):
            cols = slice(g * LANES, (g + 1) * LANES)
            scores = pair_products(
                q_ref[i * BLK : (i + 2) * BLK, cols], k_ref[i * BLK : (i + 4) * BLK, cols], masks, masks2, per
            )
            for t in range(2):
                outer_cols, shared_cols = window_parts(t)
                parts = []
                for h in range(per):
                    gam = gam_ref[layer, g * per + h] * LOG2E
                    outer, shared = scores[t][h]
                    outer = outer - gam * d2_ref[d2_first + i + t, :, outer_cols]
                    shared = shared - gam * d2_ref[d2_first + i + t, :, shared_cols]
                    peak = jnp.maximum(jnp.maximum(outer, shared[:, :BLK]), shared[:, BLK:])
                    peak = jnp.max(peak, axis=1, keepdims=True)
                    outer = jnp.exp2(outer - peak).astype(BF16)
                    shared = jnp.exp2(shared - peak).astype(BF16)
                    e = jnp.concatenate([outer, shared] if t == 0 else [shared, outer], axis=1)
                    e_ref[i + t, g * per + h] = e
                    parts.append(e)
                rows = slice((i + t) * BLK, (i + t + 1) * BLK)
                v = v_ref[(i + t) * BLK : (i + t + 3) * BLK, cols]
                out = mm(jnp.concatenate(parts, axis=1), jnp.concatenate([stacked(v, masks3), ones], axis=1))
                rl = 1.0 / out[:, LANES:]
                rl_ref[rows, cols] = rl
                o_ref[rows, cols] = (out[:, :LANES] * rl).astype(BF16)


def delta_of(prod, per, hdim):
    lane = lax.broadcasted_iota(jnp.int32, prod.shape, 1) // hdim
    return [jnp.sum(jnp.where(lane == h, prod, 0.0), axis=1, keepdims=True) for h in range(per)]


def fold(grad, ext, ext_t, qb, kb):
    cols, rows = [], []
    for c in range(3):
        diff = ext_t[qb * BLK : (qb + 1) * BLK, c : c + 1] - ext[c : c + 1, kb * BLK : (kb + 1) * BLK]
        t = grad * diff
        cols.append(2.0 * jnp.sum(t, axis=1, keepdims=True))
        rows.append(-2.0 * jnp.sum(t, axis=0, keepdims=True))
    return cols, rows


def columns_to_rows(cols):
    lane = lax.broadcasted_iota(jnp.int32, (BLK, LANES), 1)
    wide = jnp.zeros((BLK, LANES), F32)
    for c in range(3):
        wide = jnp.where(lane == c, cols[c], wide)
    return wide.T[:8]


def three_rows(rows):
    sub = lax.broadcasted_iota(jnp.int32, (8, LANES), 0)
    out = jnp.zeros((8, LANES), F32)
    for c in range(3):
        out = jnp.where(sub == c, rows[c], out)
    return out


def pack_kernel(nb, me_ref, list_ref, pos_ref, spec_ref, own_ref):
    own_ref[...] = jnp.zeros_like(own_ref)
    own_ref[0:3] = pos_ref[...]
    own_ref[3:4] = spec_ref[...].astype(F32)
    for b in range(nb):
        for s in range(3):
            listed = list_ref[b, s]
            ok = jnp.logical_and(listed == me_ref[0] * nb + (b - 1 + s), listed >= 0)
            own_ref[4 + s : 5 + s, b * BLK : (b + 1) * BLK] = jnp.full((1, BLK), ok.astype(F32))


def first_kernel(
    nb, heads, hdim,
    me_ref, gam_ref, own_ref, ra_ref, rb_ref, embed_ref, gains_ref, outg_ref, ro_ref,
    wq_h, wk_h, wv_h, wo_h, wu_h, wd_h,
    e_out, ext_ref, gk_ref, o_ref, rl_ref, v_ref, x1_ref, gd_ref, e_ref, wo0, wu0, wd0,
    st_ref, q1_ref, k1_ref, v1_ref, o1_ref, rl1_ref, e1_ref, x11_ref, gd1_ref, top_ref, wq1, wk1, wv1, wo1, wu1, wd1,
    wq0, wk0, wv0, d2_ref, x0_ref, q_ref, k_ref, sem,
):
    qb = nb + 2
    kb = nb + 4
    mid = slice(BLK, (nb + 1) * BLK)
    sources = (wq_h, wk_h, wv_h, wo_h, wu_h, wd_h)
    targets = ((wq0, wk0, wv0, wo0, wu0, wd0), (wq1, wk1, wv1, wo1, wu1, wd1))
    copies = []
    for layer in range(2):
        copies.append([
            pltpu.make_async_copy(src.at[layer], dst, sem.at[layer, n])
            for n, (src, dst) in enumerate(zip(sources, targets[layer]))
        ])
        for c in copies[layer]:
            c.start()
    par = lax.rem(me_ref[0], 2)
    before, own, after = arrange(par, own_ref[...], ra_ref[...], rb_ref[...])
    ext = jnp.concatenate([before, own, after], axis=1)
    ext_ref[...] = ext
    gk_ref[...] = gains_ref[...]
    ext_t = ext.T
    distances(ext, ext_t, 1, d2_ref, qb)

    embed = embed_ref[...].astype(F32)
    normed = (embed * inv_rms(embed) * gains_ref[0, 0:1]).astype(BF16)
    scale = hdim ** (-0.5)
    spec = ext_t[:, 3:4].astype(jnp.int32)
    nspec = embed_ref.shape[0]
    onehot = (spec == lax.broadcasted_iota(jnp.int32, (kb * BLK, nspec), 1)).astype(F32).astype(BF16)
    onehot_q = onehot[BLK : (qb + 1) * BLK]
    x0_ref[...] = mm(onehot_q, embed_ref[...])
    for c in copies[0][:3]:
        c.wait()
    q_ref[...] = mm(onehot_q, (mm(normed, wq0[...]) * (scale * LOG2E)).astype(BF16)).astype(BF16)
    k_ref[...] = mm(onehot, mm(normed, wk0[...]).astype(BF16)).astype(BF16)
    v_ref[...] = mm(onehot, mm(normed, wv0[...]).astype(BF16)).astype(BF16)
    attend(q_ref, k_ref, v_ref, o_ref, rl_ref, e_ref, d2_ref, 0, gam_ref, 0, heads, hdim, qb)

    for c in copies[0][3:]:
        c.wait()

    def feed(layer, x1, w_up, w_down, keep):
        inner = (x1 * inv_rms(x1) * gains_ref[layer, 1:2]).astype(BF16)
        act, slope = gelu_both(mm(inner, w_up[...]))
        keep(slope.astype(BF16))
        return x1 + mm(act.astype(BF16), w_down[...])

    step = 2 * BLK
    for r in range(0, qb * BLK, step):
        rows = slice(r, r + step)
        x1 = x0_ref[rows] + mm(o_ref[rows], wo0[...])
        x1_ref[rows] = x1
        st_ref[rows] = feed(0, x1, wu0, wd0, lambda slope: gd_ref.__setitem__(rows, slope))

    for c in copies[1]:
        c.wait()
    gain = gains_ref[1, 0:1]
    st = st_ref[...]
    normed = (st * inv_rms(st) * gain).astype(BF16)
    q1_ref[...] = (mm(normed[mid], wq1[...]) * (scale * LOG2E)).astype(BF16)
    k1_ref[...] = mm(normed, wk1[...]).astype(BF16)
    v1_ref[...] = mm(normed, wv1[...]).astype(BF16)
    attend(q1_ref, k1_ref, v1_ref, o1_ref, rl1_ref, e1_ref, d2_ref, 1, gam_ref, 1, heads, hdim, nb)
    x1 = st_ref[mid] + mm(o1_ref[...], wo1[...])
    x11_ref[...] = x1
    x2 = feed(1, x1, wu1, wd1, lambda slope: gd1_ref.__setitem__(..., slope))

    w = outg_ref[...] * ro_ref[...]
    r = inv_rms(x2)
    along = jnp.sum(x2 * w, axis=1, keepdims=True)
    e_out[...] = jnp.broadcast_to(jnp.sum(along * r), e_out.shape)
    width = x2.shape[1]
    top_ref[...] = r * (w - x2 * (r * r * along * (1.0 / width)))


def middle_kernel(
    nb, heads, hdim,
    me_ref, gam_ref, _, ext_ref, gains_ref, st_ref, q1_ref, k1_ref, v1_ref, o1_ref, rl1_ref, e1_ref, x1_ref, gd_ref, top_ref,
    wq, wk, wv, wo, wu, wd,
    paya_ref, payb_ref, part_ref, halo_ref, g1_ref,
    dq_ref, dk_ref, dv_ref, datt_ref,
):
    qb = nb + 2
    mid = slice(BLK, (nb + 1) * BLK)
    scale = hdim ** (-0.5)
    width = st_ref.shape[1]
    par = lax.rem(me_ref[0], 2)
    ext = ext_ref[...]
    ext_t = ext.T
    grad = top_ref[...]
    du = mm_nt(grad.astype(BF16), wd[...]).astype(BF16).astype(F32)
    dinner = mm_nt((du * gd_ref[...].astype(F32)).astype(BF16), wu[...]).astype(BF16).astype(F32)
    grad = grad + rms_back(x1_ref[...], gains_ref[1, 1:2], dinner)
    datt_ref[...] = mm_nt(grad.astype(BF16), wo[...]).astype(BF16).astype(F32)

    per = LANES // hdim
    groups = heads // per
    masks = head_masks(BLK, per, hdim)
    masks2 = head_masks(2 * BLK, per, hdim)
    masks3 = head_masks(3 * BLK, per, hdim)
    dk_ref[...] = jnp.zeros_like(dk_ref)
    dv_ref[...] = jnp.zeros_like(dv_ref)
    g1_ref[...] = jnp.zeros_like(g1_ref)
    for i in range(0, nb, 2):
        rows2 = slice(i * BLK, (i + 2) * BLK)
        for g in range(groups):
            cols = slice(g * LANES, (g + 1) * LANES)
            d_o = datt_ref[rows2, cols] * rl1_ref[rows2, cols]
            delta = delta_of(d_o * o1_ref[rows2, cols].astype(F32), per, hdim)
            d_o = d_o.astype(BF16)
            prods = pair_products(d_o, v1_ref[i * BLK : (i + 4) * BLK, cols], masks, masks2, per)
            for t in range(2):
                at = slice(t * BLK, (t + 1) * BLK)
                rows = slice((i + t) * BLK, (i + t + 1) * BLK)
                win = slice((i + t) * BLK, (i + t + 3) * BLK)
                outer_cols, shared_cols = window_parts(t)
                dos = stacked(d_o[at], masks)
                qs = stacked(q1_ref[rows, cols], masks)
                parts, es = [], []
                pair_outer = g1_ref[i + t, :, outer_cols]
                pair_shared = g1_ref[i + t, :, shared_cols]
                for h in range(per):
                    e = e1_ref[i + t, g * per + h]
                    outer, shared = prods[t][h]
                    gam = gam_ref[1, g * per + h]
                    outer = e[:, outer_cols].astype(F32) * (outer - delta[h][at])
                    shared = e[:, shared_cols].astype(F32) * (shared - delta[h][at])
                    pair_outer = pair_outer + gam * outer
                    pair_shared = pair_shared + gam * shared
                    outer, shared = outer.astype(BF16), shared.astype(BF16)
                    parts.append(jnp.concatenate([outer, shared] if t == 0 else [shared, outer], axis=1))
                    es.append(e)
                g1_ref[i + t, :, outer_cols] = pair_outer
                g1_ref[i + t, :, shared_cols] = pair_shared
                ks = stacked(k1_ref[win, cols], masks3)
                dq_ref[rows, cols] = (mm(jnp.concatenate(parts, axis=1), ks) * scale).astype(BF16)
                dk_ref[win, cols] += mm_tn(jnp.concatenate(parts, axis=0), qs)
                dv_ref[win, cols] += mm_tn(jnp.concatenate(es, axis=0), dos)
    dk = (dk_ref[...] * LN2).astype(BF16)
    dv = dv_ref[...].astype(BF16)
    dnorm = mm_nt(dk, wk[...]) + mm_nt(dv, wv[...])
    dq = mm_nt(dq_ref[...], wq[...])
    zeros = jnp.zeros((BLK, width), F32)
    dnorm = dnorm + jnp.concatenate([zeros, dq, zeros], axis=0)
    back = rms_back(st_ref[...], gains_ref[1, 0:1], dnorm.astype(BF16).astype(F32))
    part = grad + back[mid]
    part_ref[...] = part
    halo_ref[:BLK] = back[:BLK]
    halo_ref[BLK:] = back[(qb - 1) * BLK :]

    _, rows_low = fold(g1_ref[0, :, :BLK], ext, ext_t, 2, 1)
    _, rows_high = fold(g1_ref[nb - 1, :, 2 * BLK :], ext, ext_t, nb + 1, nb + 2)
    pad = jnp.zeros((8, width - LANES), F32)

    def payload(ref, halo, edge, rows):
        ref[:BLK] = halo.astype(BF16)
        ref[BLK : 2 * BLK] = edge.astype(BF16)
        tail = jnp.concatenate([three_rows(rows), pad], axis=1)
        ref[2 * BLK :] = jnp.concatenate([tail, jnp.zeros_like(tail)], axis=0).astype(BF16)

    def low(ref):
        payload(ref, back[:BLK], part[:BLK], rows_low)

    def high(ref):
        payload(ref, back[(qb - 1) * BLK :], part[(nb - 1) * BLK :], rows_high)

    @pl.when(par == 0)
    def _():
        high(paya_ref)
        low(payb_ref)

    @pl.when(par != 0)
    def _():
        low(paya_ref)
        high(payb_ref)


def last_kernel(
    nb, heads, hdim,
    me_ref, gam_ref, _, ext_ref, gains_ref, paya_ref, payb_ref, part_ref, halo_ref, g1_ref,
    o_ref, rl_ref, v_ref, x1_ref, gd_ref, e_ref, wo, wu, wd,
    f_ref,
    datt_ref,
):
    qb = nb + 2
    par = lax.rem(me_ref[0], 2)
    ext = ext_ref[...]
    ext_t = ext.T
    from_low, _, from_high = arrange(par, None, paya_ref[...], payb_ref[...])
    from_low = from_low.astype(F32)
    from_high = from_high.astype(F32)
    part = part_ref[...]
    pieces = [halo_ref[:BLK] + from_low[BLK : 2 * BLK]]
    own_parts = [part[i * BLK : (i + 1) * BLK] for i in range(nb)]
    own_parts[0] = own_parts[0] + from_low[:BLK]
    own_parts[-1] = own_parts[-1] + from_high[:BLK]
    pieces += own_parts
    pieces.append(halo_ref[BLK:] + from_high[BLK : 2 * BLK])
    grad = jnp.concatenate(pieces, axis=0)
    du = mm_nt(grad.astype(BF16), wd[...]).astype(BF16).astype(F32)
    dinner = mm_nt((du * gd_ref[...].astype(F32)).astype(BF16), wu[...]).astype(BF16).astype(F32)
    grad = grad + rms_back(x1_ref[...], gains_ref[0, 1:2], dinner)
    datt_ref[...] = mm_nt(grad.astype(BF16), wo[...]).astype(BF16).astype(F32)

    per = LANES // hdim
    groups = heads // per
    masks = head_masks(BLK, per, hdim)
    masks2 = head_masks(2 * BLK, per, hdim)

    def cotangents(rows, cols):
        d_o = datt_ref[rows, cols] * rl_ref[rows, cols]
        return d_o.astype(BF16), delta_of(d_o * o_ref[rows, cols].astype(F32), per, hdim)

    forces = [jnp.zeros((8, LANES), F32) for _ in range(nb)]
    forces[0] = forces[0] + from_low[2 * BLK : 2 * BLK + 8, :LANES]
    forces[-1] = forces[-1] + from_high[2 * BLK : 2 * BLK + 8, :LANES]
    for i in range(0, nb, 2):
        rows2 = slice((i + 1) * BLK, (i + 3) * BLK)
        parts = [[g1_ref[i + t, :, c] for c in window_parts(t)] for t in range(2)]
        for g in range(groups):
            cols = slice(g * LANES, (g + 1) * LANES)
            d_o, delta = cotangents(rows2, cols)
            prods = pair_products(d_o, v_ref[(i + 1) * BLK : (i + 5) * BLK, cols], masks, masks2, per)
            for t in range(2):
                at = slice(t * BLK, (t + 1) * BLK)
                for h in range(per):
                    gam = gam_ref[0, g * per + h]
                    for n, c in enumerate(window_parts(t)):
                        e = e_ref[i + t + 1, g * per + h, :, c].astype(F32)
                        parts[t][n] = parts[t][n] + gam * (e * (prods[t][h][n] - delta[h][at]))
        for t in range(2):
            outer, shared = parts[t]
            total = jnp.concatenate([outer, shared] if t == 0 else [shared, outer], axis=1)
            sums = None
            for s in range(3):
                cols, rows = fold(total[:, s * BLK : (s + 1) * BLK], ext, ext_t, i + t + 2, i + t + 1 + s)
                sums = cols if sums is None else [a + b for a, b in zip(sums, cols)]
                j = i + t - 1 + s
                if 0 <= j < nb:
                    forces[j] = forces[j] + three_rows(rows)
            forces[i + t] = forces[i + t] + columns_to_rows(sums)
    last = qb - 1
    ends = [jnp.zeros((BLK, BLK), F32), jnp.zeros((BLK, BLK), F32)]
    for g in range(groups):
        cols = slice(g * LANES, (g + 1) * LANES)
        low_o, low_delta = cotangents(slice(0, BLK), cols)
        high_o, high_delta = cotangents(slice(last * BLK, qb * BLK), cols)
        both = jnp.concatenate([low_o, high_o], axis=1)
        both = jnp.concatenate([both * jnp.concatenate([m, m], axis=1) for m in masks], axis=0)
        prods = mm_nt(both, beside(v_ref[2 * BLK : 3 * BLK, cols], v_ref[last * BLK : qb * BLK, cols]))
        for h in range(per):
            gam = gam_ref[0, g * per + h]
            low = prods[h * BLK : (h + 1) * BLK, :BLK] - low_delta[h]
            high = prods[h * BLK : (h + 1) * BLK, BLK:] - high_delta[h]
            ends[0] = ends[0] + gam * (e_ref[0, g * per + h, :, 2 * BLK :].astype(F32) * low)
            ends[1] = ends[1] + gam * (e_ref[last, g * per + h, :, :BLK].astype(F32) * high)
    _, rows = fold(ends[0], ext, ext_t, 1, 2)
    forces[0] = forces[0] + three_rows(rows)
    _, rows = fold(ends[1], ext, ext_t, nb + 2, nb + 1)
    forces[-1] = forces[-1] + three_rows(rows)
    f_ref[...] = jnp.concatenate(forces, axis=1)[:3]


def swap_a(x):
    n = lax.axis_size("chain")
    return lax.ppermute(x, "chain", [(i, i ^ 1) for i in range(n)])


def swap_b(x):
    n = lax.axis_size("chain")
    return lax.ppermute(x, "chain", [(i, ((i + 1) ^ 1) - 1) for i in range(1, n - 1)])


def hop(x, step):
    return lax.ppermute(x, "chain", [(i, i ^ step) for i in range(lax.axis_size("chain"))])


def local(
    species, positions, block_list, embed, w_query, w_key, w_value, w_out, w_up, w_down, norm_gains, gammas, out_gain, readout
):
    atoms = species.shape[0]
    nb = atoms // BLK
    width = embed.shape[1]
    layers, heads = gammas.shape
    hdim = width // heads
    ff = w_up.shape[2]
    qb, kb = nb + 2, nb + 4
    count = lax.axis_size("chain")
    assert nb >= 2 and layers == 2 and LANES % hdim == 0 and nb % 2 == 0 and count >= 8 and count & (count - 1) == 0
    me = lax.axis_index("chain").astype(jnp.int32)
    vm = pltpu.VMEM
    smem = pl.BlockSpec(memory_space=pltpu.SMEM)

    def work(products):
        return pl.CostEstimate(flops=products * atoms * width * width * 8, transcendentals=0, bytes_accessed=0)

    vmem = pl.BlockSpec(memory_space=vm)
    keep = functools.partial(pltpu.with_memory_space_constraint, memory_space=vm)
    place = me.reshape(1)
    own = pl.pallas_call(
        functools.partial(pack_kernel, nb),
        out_shape=vm((8, atoms), F32),
        in_specs=[smem, smem, vmem, vmem],
        out_specs=vmem,
    )(place, block_list, positions, species.reshape(1, atoms))
    edge = 2 * BLK
    if atoms == edge:
        send_a = send_b = own
    else:
        first, last = own[:, :edge], own[:, -edge:]
        send_a = jnp.where(me % 2 == 0, last, first)
        send_b = jnp.where(me % 2 == 0, first, last)
    near_a, near_b = swap_a(send_a), swap_b(send_b)
    pin = functools.partial(pltpu.with_memory_space_constraint, memory_space=pltpu.HBM)
    weights = (w_query, w_key, w_value, w_out, w_up, w_down)
    shapes = [vm((width, width), BF16)] * 4 + [vm((width, ff), BF16), vm((ff, width), BF16)]
    first = pl.pallas_call(
        functools.partial(first_kernel, nb, heads, hdim),
        out_shape=[
            vm((8, LANES), F32), vm((8, kb * BLK), F32), vm(norm_gains.shape, F32),
            vm((qb * BLK, width), BF16), vm((qb * BLK, width), F32), vm((kb * BLK, width), BF16),
            vm((qb * BLK, width), F32), vm((qb * BLK, ff), BF16), vm((qb, heads, BLK, 3 * BLK), BF16), *shapes[3:],
            vm((qb * BLK, width), F32), vm((nb * BLK, width), BF16), vm((qb * BLK, width), BF16),
            vm((qb * BLK, width), BF16), vm((nb * BLK, width), BF16), vm((nb * BLK, width), F32),
            vm((nb, heads, BLK, 3 * BLK), BF16), vm((nb * BLK, width), F32), vm((nb * BLK, ff), BF16),
            vm((nb * BLK, width), F32), *shapes,
        ],
        in_specs=[smem, smem] + [vmem] * 7 + [pl.BlockSpec(memory_space=pltpu.HBM)] * 6,
        out_specs=[vmem] * 28,
        scratch_shapes=[
            *shapes[:3], vm((qb, BLK, 3 * BLK), F32), vm((qb * BLK, width), F32), vm((qb * BLK, width), BF16),
            vm((kb * BLK, width), BF16), pltpu.SemaphoreType.DMA((2, 6)),
        ],
        compiler_params=pltpu.CompilerParams(vmem_limit_bytes=20 * 1024 * 1024),
        cost_estimate=work(qb * 7),
    )(
        place, gammas, keep(own), keep(near_a), keep(near_b), pin(embed), pin(norm_gains),
        pin(out_gain.reshape(1, width)), pin(readout.reshape(1, width)), *(pin(w) for w in weights),
    )
    energy, ext, gains = first[0], keep(first[1]), keep(first[2])
    saved0 = [keep(x) for x in first[3:12]]
    saved1 = [keep(x) for x in first[12:]]
    energy = energy + hop(energy, 1)
    pay = vm((2 * BLK + 16, width), BF16)
    pay_a, pay_b, part, halo, pairs = pl.pallas_call(
        functools.partial(middle_kernel, nb, heads, hdim),
        out_shape=[pay, pay, vm((nb * BLK, width), F32), vm((2 * BLK, width), F32), vm((nb, BLK, 3 * BLK), F32)],
        in_specs=[smem, smem] + [vmem] * 19,
        out_specs=[vmem] * 5,
        scratch_shapes=[
            vm((nb * BLK, width), BF16), vm((qb * BLK, width), F32), vm((qb * BLK, width), F32), vm((nb * BLK, width), F32),
        ],
        compiler_params=pltpu.CompilerParams(vmem_limit_bytes=20 * 1024 * 1024),
        cost_estimate=work(nb * 9),
    )(place, gammas, keep(energy), ext, gains, *saved1)
    energy = energy + hop(energy, 2)
    energy, pay_a, pay_b = lax.optimization_barrier((energy, pay_a, pay_b))
    arriving = hop(energy, 4)
    got_a, got_b = swap_a(pay_a), swap_b(pay_b)
    energy = energy + arriving
    forces = pl.pallas_call(
        functools.partial(last_kernel, nb, heads, hdim),
        out_shape=jax.ShapeDtypeStruct((3, atoms), F32),
        in_specs=[smem, smem] + [vmem] * 17,
        out_specs=vmem,
        scratch_shapes=[vm((qb * BLK, width), F32)],
        compiler_params=pltpu.CompilerParams(vmem_limit_bytes=20 * 1024 * 1024),
        cost_estimate=work(qb * 3),
    )(
        place, gammas, keep(energy), ext, gains, keep(got_a), keep(got_b), keep(part), keep(halo), keep(pairs), *saved0
    )
    if count > 8:
        arriving = hop(energy, 8)
        energy, forces = lax.optimization_barrier((energy, forces))
        energy = energy + arriving
    step = 16
    while step < count:
        energy = energy + hop(energy, step)
        step *= 2
    return energy[:1, :1].reshape(1), forces


def solution(mesh):
    sharded = ("frames", "chain")
    return jax.shard_map(
        local,
        mesh=mesh,
        in_specs=(P(sharded), P(None, sharded), P(sharded, None)) + (P(),) * 11,
        out_specs=(P("frames"), P(None, sharded)),
        check_vma=False,
    )
```

```python
import functools
import math

import jax
import jax.numpy as jnp
from jax import lax
from jax.experimental import pallas as pl
from jax.experimental.pallas import tpu as pltpu
from jax.sharding import PartitionSpec as P

BLK = 128
LANES = 128
EPS = 1e-06
LOG2E = math.log2(math.e)
LN2 = math.log(2.0)
FAR = 1e30
F32 = jnp.float32
BF16 = jnp.bfloat16
C0 = math.sqrt(2.0 / math.pi)
C1 = 0.044715


def mm(a, b):
    return jnp.dot(a, b, preferred_element_type=F32)


def mm_nt(a, b):
    return lax.dot_general(a, b, (((1,), (1,)), ((), ())), preferred_element_type=F32)


def mm_tn(a, b):
    return lax.dot_general(a, b, (((0,), (0,)), ((), ())), preferred_element_type=F32)


def inv_rms(x):
    return lax.rsqrt(jnp.mean(x * x, axis=-1, keepdims=True) + EPS)


def rms_back(x, gain, cot):
    r = inv_rms(x)
    t = cot * gain
    return r * (t - x * (r * r * jnp.mean(x * t, axis=-1, keepdims=True)))


def gelu_both(x):
    sq = x * x
    half = 0.5 + 0.5 * jnp.tanh(x * (C0 + (C0 * C1) * sq))
    act = x * half
    return act, half + act * (1.0 - half) * (2.0 * C0 + (6.0 * C0 * C1) * sq)


def head_masks(rows, heads_per_group, hdim):
    lane = lax.broadcasted_iota(jnp.int32, (rows, LANES), 1) // hdim
    return [(lane == h).astype(F32).astype(BF16) for h in range(heads_per_group)]


def arrange(par, own, from_a, from_b):
    before = jnp.where(par == 0, from_b, from_a)
    after = jnp.where(par == 0, from_a, from_b)
    return before, own, after


def distances(ext, ext_t, first, d2_ref, count):
    for i in range(count):
        q = ext_t[(first + i) * BLK : (first + i + 1) * BLK]
        for s in range(3):
            k0 = (first + i - 1 + s) * BLK
            tot = None
            for c in range(3):
                diff = q[:, c : c + 1] - ext[c : c + 1, k0 : k0 + BLK]
                tot = diff * diff if tot is None else tot + diff * diff
            d2_ref[i, :, s * BLK : (s + 1) * BLK] = jnp.where(q[:, 4 + s : 5 + s] > 0.5, tot, FAR)


def stacked(x, masks):
    return jnp.concatenate([x * m for m in masks], axis=0)


def beside(x, y):
    zero = jnp.zeros_like(x)
    return jnp.concatenate([jnp.concatenate([x, zero], axis=1), jnp.concatenate([zero, y], axis=1)], axis=0)


def pair_products(a, b, masks2, per):
    each = [a * m for m in masks2]
    shared = mm_nt(jnp.concatenate(each, axis=0), b[BLK : 3 * BLK])
    both = jnp.concatenate([jnp.concatenate([x[:BLK], x[BLK:]], axis=1) for x in each], axis=0)
    outer = mm_nt(both, beside(b[:BLK], b[3 * BLK :]))
    got = []
    for t in range(2):
        got.append([
            (outer[h * BLK : (h + 1) * BLK, t * BLK : (t + 1) * BLK], shared[(2 * h + t) * BLK : (2 * h + t + 1) * BLK])
            for h in range(per)
        ])
    return got, each


def span(first, size, unit):
    if isinstance(first, int):
        return slice(first * unit, first * unit + size)
    return pl.ds(pl.multiple_of(first * unit, unit), size)


def blocks_at(first, count):
    return span(first, count * BLK, BLK)


def group_at(g):
    return span(g, LANES, LANES)


def over(pairs, groups, body, rolled=False):
    if rolled:
        lax.fori_loop(0, pairs * groups, lambda n, _: (body(2 * lax.div(n, groups), lax.rem(n, groups)), 0)[1], 0)
    else:
        for n in range(pairs * groups):
            body(2 * (n // groups), n % groups)


def window_parts(t):
    return (slice(0, BLK), slice(BLK, 3 * BLK)) if t == 0 else (slice(2 * BLK, 3 * BLK), slice(0, 2 * BLK))


def head_norms(x, hdim):
    width = x.shape[1]
    lane = lax.broadcasted_iota(jnp.int32, (width, LANES), 0) // hdim
    member = (lane == lax.broadcasted_iota(jnp.int32, (width, LANES), 1)).astype(F32).astype(BF16)
    x = x.astype(F32)
    return jnp.max(mm((x * x).astype(BF16), member), axis=0, keepdims=True)


def small_scores(q, k, hdim):
    return jnp.max(head_norms(q, hdim) * head_norms(k, hdim)) < 3600.0


def attend(exact, q_ref, k_ref, vm_ref, o_ref, rl_ref, e_ref, d2_ref, d2_first, gam_ref, layer, heads, hdim, count):
    per = LANES // hdim
    groups = heads // per
    masks2 = head_masks(2 * BLK, per, hdim)
    ones2 = jnp.concatenate(masks2, axis=0)
    ones1 = jnp.concatenate([m[:BLK] for m in masks2], axis=0)

    def values(first, blocks, cols, ones):
        rows = blocks_at(first, blocks)
        return jnp.concatenate([jnp.concatenate([vm_ref[h, rows, cols] for h in range(per)], axis=0), ones], axis=1)

    def body(i, g):
        cols = group_at(g)
        scores, _ = pair_products(q_ref[blocks_at(i, 2), cols], k_ref[blocks_at(i, 4), cols], masks2, per)
        sides, middles = [], []
        for t in range(2):
            outer_cols, shared_cols = window_parts(t)
            outers, shareds = [], []
            for h in range(per):
                gam = gam_ref[layer, g * per + h] * LOG2E
                outer, shared = scores[t][h]
                outer = outer - gam * d2_ref[d2_first + i + t, :, outer_cols]
                shared = shared - gam * d2_ref[d2_first + i + t, :, shared_cols]
                if exact:
                    peak = jnp.maximum(jnp.maximum(outer, shared[:, :BLK]), shared[:, BLK:])
                    peak = jnp.max(peak, axis=1, keepdims=True)
                    outer, shared = outer - peak, shared - peak
                outer = jnp.exp2(outer).astype(BF16)
                shared = jnp.exp2(shared).astype(BF16)
                e_ref[i + t, g * per + h, :, outer_cols] = outer
                e_ref[i + t, g * per + h, :, shared_cols] = shared
                outers.append(outer)
                shareds.append(shared)
            middles.append(jnp.concatenate(shareds, axis=1))
            sides.append(mm(jnp.concatenate(outers, axis=1), values(i + 3 * t, 1, cols, ones1)))
        out = mm(jnp.concatenate(middles, axis=0), values(i + 1, 2, cols, ones2)) + jnp.concatenate(sides, axis=0)
        rl = 1.0 / jnp.maximum(out[:, LANES:], 1e-37)
        rl_ref[blocks_at(i, 2), cols] = rl
        o_ref[blocks_at(i, 2), cols] = (out[:, :LANES] * rl).astype(BF16)

    over(count // 2, groups, body, rolled=exact)


def split_heads(v_ref, vm_ref, hdim):
    rows, width = v_ref.shape
    masks = head_masks(BLK, LANES // hdim, hdim)
    for r in range(0, rows, BLK):
        for c in range(0, width, LANES):
            for h, m in enumerate(masks):
                vm_ref[h, r : r + BLK, c : c + LANES] = v_ref[r : r + BLK, c : c + LANES] * m


def delta_of(prod, per, hdim):
    lane = lax.broadcasted_iota(jnp.int32, prod.shape, 1) // hdim
    return [jnp.sum(jnp.where(lane == h, prod, 0.0), axis=1, keepdims=True) for h in range(per)]


def fold(grad, ext, ext_t, qb, kb):
    cols, rows = [], []
    for c in range(3):
        diff = ext_t[qb * BLK : (qb + 1) * BLK, c : c + 1] - ext[c : c + 1, kb * BLK : (kb + 1) * BLK]
        t = grad * diff
        cols.append(2.0 * jnp.sum(t, axis=1, keepdims=True))
        rows.append(-2.0 * jnp.sum(t, axis=0, keepdims=True))
    return cols, rows


def columns_to_rows(cols):
    lane = lax.broadcasted_iota(jnp.int32, (BLK, LANES), 1)
    wide = jnp.zeros((BLK, LANES), F32)
    for c in range(3):
        wide = jnp.where(lane == c, cols[c], wide)
    return wide.T[:8]


def three_rows(rows):
    sub = lax.broadcasted_iota(jnp.int32, (8, LANES), 0)
    out = jnp.zeros((8, LANES), F32)
    for c in range(3):
        out = jnp.where(sub == c, rows[c], out)
    return out


def pack_kernel(nb, me_ref, list_ref, pos_ref, spec_ref, own_ref):
    own_ref[...] = jnp.zeros_like(own_ref)
    own_ref[0:3] = pos_ref[...]
    own_ref[3:4] = spec_ref[...].astype(F32)
    for b in range(nb):
        for s in range(3):
            listed = list_ref[b, s]
            ok = jnp.logical_and(listed == me_ref[0] * nb + (b - 1 + s), listed >= 0)
            own_ref[4 + s : 5 + s, b * BLK : (b + 1) * BLK] = jnp.full((1, BLK), ok.astype(F32))


def first_kernel(
    nb, heads, hdim,
    me_ref, gam_ref, own_ref, ra_ref, rb_ref, embed_ref, gains_ref, outg_ref, ro_ref,
    wq_h, wk_h, wv_h, wo_h, wu_h, wd_h,
    e_out, ext_ref, gk_ref, o_ref, rl_ref, v_ref, x1_ref, gd_ref, e_ref, wo0, wu0, wd0,
    st_ref, q1_ref, k1_ref, v1_ref, o1_ref, rl1_ref, e1_ref, x11_ref, gd1_ref, top_ref, wq1, wk1, wv1, wo1, wu1, wd1,
    wq0, wk0, wv0, d2_ref, x0_ref, q_ref, k_ref, vm_ref, vm1_ref, sem,
):
    qb = nb + 2
    kb = nb + 4
    mid = slice(BLK, (nb + 1) * BLK)
    sources = (wq_h, wk_h, wv_h, wo_h, wu_h, wd_h)
    targets = ((wq0, wk0, wv0, wo0, wu0, wd0), (wq1, wk1, wv1, wo1, wu1, wd1))
    copies = []
    for layer in range(2):
        copies.append([
            pltpu.make_async_copy(src.at[layer], dst, sem.at[layer, n])
            for n, (src, dst) in enumerate(zip(sources, targets[layer]))
        ])
        for c in copies[layer]:
            c.start()
    par = lax.rem(me_ref[0], 2)
    before, own, after = arrange(par, own_ref[...], ra_ref[...], rb_ref[...])
    ext = jnp.concatenate([before, own, after], axis=1)
    ext_ref[...] = ext
    gk_ref[...] = gains_ref[...]
    ext_t = ext.T
    distances(ext, ext_t, 1, d2_ref, qb)

    embed = embed_ref[...].astype(F32)
    normed = (embed * inv_rms(embed) * gains_ref[0, 0:1]).astype(BF16)
    scale = hdim ** (-0.5)
    spec = ext_t[:, 3:4].astype(jnp.int32)
    nspec = embed_ref.shape[0]
    onehot = (spec == lax.broadcasted_iota(jnp.int32, (kb * BLK, nspec), 1)).astype(F32).astype(BF16)
    onehot_q = onehot[BLK : (qb + 1) * BLK]
    x0_ref[...] = mm(onehot_q, embed_ref[...])
    for c in copies[0][:3]:
        c.wait()
    q_table = (mm(normed, wq0[...]) * (scale * LOG2E)).astype(BF16)
    q_ref[...] = mm(onehot_q, q_table).astype(BF16)
    k_table = mm(normed, wk0[...]).astype(BF16)
    k_ref[...] = mm(onehot, k_table).astype(BF16)
    v_ref[...] = mm(onehot, mm(normed, wv0[...]).astype(BF16)).astype(BF16)
    split_heads(v_ref, vm_ref, hdim)

    def run(exact):
        def arrived(some):
            if not exact:
                for c in some:
                    c.wait()

        attend(exact, q_ref, k_ref, vm_ref, o_ref, rl_ref, e_ref, d2_ref, 0, gam_ref, 0, heads, hdim, qb)

        arrived(copies[0][3:])

        def feed(layer, x1, w_up, w_down, keep):
            inner = (x1 * inv_rms(x1) * gains_ref[layer, 1:2]).astype(BF16)
            act, slope = gelu_both(mm(inner, w_up[...]))
            keep(slope.astype(BF16))
            return x1 + mm(act.astype(BF16), w_down[...])

        step = 4 * BLK
        for r in range(0, qb * BLK, step):
            rows = slice(r, r + step)
            x1 = x0_ref[rows] + mm(o_ref[rows], wo0[...])
            x1_ref[rows] = x1
            st_ref[rows] = feed(0, x1, wu0, wd0, lambda slope: gd_ref.__setitem__(rows, slope))

        arrived(copies[1])
        gain = gains_ref[1, 0:1]
        st = st_ref[...]
        normed = (st * inv_rms(st) * gain).astype(BF16)
        q1_ref[...] = (mm(normed[mid], wq1[...]) * (scale * LOG2E)).astype(BF16)
        k1_ref[...] = mm(normed, wk1[...]).astype(BF16)
        v1_ref[...] = mm(normed, wv1[...]).astype(BF16)
        split_heads(v1_ref, vm1_ref, hdim)
        attend(exact, q1_ref, k1_ref, vm1_ref, o1_ref, rl1_ref, e1_ref, d2_ref, 1, gam_ref, 1, heads, hdim, nb)
        x1 = st_ref[mid] + mm(o1_ref[...], wo1[...])
        x11_ref[...] = x1
        x2 = feed(1, x1, wu1, wd1, lambda slope: gd1_ref.__setitem__(..., slope))

        w = outg_ref[...] * ro_ref[...]
        r = inv_rms(x2)
        along = jnp.sum(x2 * w, axis=1, keepdims=True)
        e_out[...] = jnp.broadcast_to(jnp.sum(along * r), e_out.shape)
        width = x2.shape[1]
        top_ref[...] = r * (w - x2 * (r * r * along * (1.0 / width)))

    run(False)
    small = jnp.logical_and(small_scores(q_table, k_table, hdim), small_scores(q1_ref[...], k1_ref[...], hdim))

    @pl.when(jnp.logical_not(small))
    def _():
        run(True)


def middle_kernel(
    nb, heads, hdim,
    me_ref, gam_ref, _, ext_ref, gains_ref, st_ref, q1_ref, k1_ref, v1_ref, o1_ref, rl1_ref, e1_ref, x1_ref, gd_ref, top_ref,
    wq, wk, wv, wo, wu, wd,
    paya_ref, payb_ref, part_ref, halo_ref, g1_ref,
    dq_ref, dk_ref, dv_ref, datt_ref,
):
    qb = nb + 2
    mid = slice(BLK, (nb + 1) * BLK)
    scale = hdim ** (-0.5)
    width = st_ref.shape[1]
    par = lax.rem(me_ref[0], 2)
    ext = ext_ref[...]
    ext_t = ext.T
    grad = top_ref[...]
    du = mm_nt(grad.astype(BF16), wd[...]).astype(BF16).astype(F32)
    dinner = mm_nt((du * gd_ref[...].astype(F32)).astype(BF16), wu[...]).astype(BF16).astype(F32)
    grad = grad + rms_back(x1_ref[...], gains_ref[1, 1:2], dinner)
    datt_ref[...] = mm_nt(grad.astype(BF16), wo[...]).astype(BF16).astype(F32)

    per = LANES // hdim
    groups = heads // per
    masks2 = head_masks(2 * BLK, per, hdim)
    masks3 = head_masks(3 * BLK, per, hdim)
    dk_ref[...] = jnp.zeros_like(dk_ref)
    dv_ref[...] = jnp.zeros_like(dv_ref)
    g1_ref[...] = jnp.zeros_like(g1_ref)

    def body(i, g):
        cols = group_at(g)
        rows2 = blocks_at(i, 2)
        d_o = datt_ref[rows2, cols] * rl1_ref[rows2, cols]
        delta = delta_of(d_o * o1_ref[rows2, cols].astype(F32), per, hdim)
        prods, each_do = pair_products(d_o.astype(BF16), v1_ref[blocks_at(i, 4), cols], masks2, per)
        q = q1_ref[rows2, cols]
        each_q = [q * m for m in masks2]
        for t in range(2):
            at = slice(t * BLK, (t + 1) * BLK)
            rows, win = blocks_at(i + t, 1), blocks_at(i + t, 3)
            outer_cols, shared_cols = window_parts(t)
            dos = jnp.concatenate([x[at] for x in each_do], axis=0)
            qs = jnp.concatenate([x[at] for x in each_q], axis=0)
            parts, es = [], []
            pair_outer = g1_ref[i + t, :, outer_cols]
            pair_shared = g1_ref[i + t, :, shared_cols]
            for h in range(per):
                e = e1_ref[i + t, g * per + h]
                outer, shared = prods[t][h]
                gam = gam_ref[1, g * per + h]
                outer = e[:, outer_cols].astype(F32) * (outer - delta[h][at])
                shared = e[:, shared_cols].astype(F32) * (shared - delta[h][at])
                pair_outer = pair_outer + gam * outer
                pair_shared = pair_shared + gam * shared
                outer, shared = outer.astype(BF16), shared.astype(BF16)
                parts.append(jnp.concatenate([outer, shared] if t == 0 else [shared, outer], axis=1))
                es.append(e)
            g1_ref[i + t, :, outer_cols] = pair_outer
            g1_ref[i + t, :, shared_cols] = pair_shared
            ks = stacked(k1_ref[win, cols], masks3)
            dq_ref[rows, cols] = (mm(jnp.concatenate(parts, axis=1), ks) * scale).astype(BF16)
            dk_ref[win, cols] += mm_tn(jnp.concatenate(parts, axis=0), qs)
            dv_ref[win, cols] += mm_tn(jnp.concatenate(es, axis=0), dos)

    over(nb // 2, groups, body)
    dk = (dk_ref[...] * LN2).astype(BF16)
    dv = dv_ref[...].astype(BF16)
    dnorm = mm_nt(dk, wk[...]) + mm_nt(dv, wv[...])
    dq = mm_nt(dq_ref[...], wq[...])
    zeros = jnp.zeros((BLK, width), F32)
    dnorm = dnorm + jnp.concatenate([zeros, dq, zeros], axis=0)
    back = rms_back(st_ref[...], gains_ref[1, 0:1], dnorm.astype(BF16).astype(F32))
    part = grad + back[mid]
    part_ref[...] = part
    halo_ref[:BLK] = back[:BLK]
    halo_ref[BLK:] = back[(qb - 1) * BLK :]

    _, rows_low = fold(g1_ref[0, :, :BLK], ext, ext_t, 2, 1)
    _, rows_high = fold(g1_ref[nb - 1, :, 2 * BLK :], ext, ext_t, nb + 1, nb + 2)
    pad = jnp.zeros((8, width - LANES), F32)

    def payload(ref, halo, edge, rows):
        ref[:BLK] = halo.astype(BF16)
        ref[BLK : 2 * BLK] = edge.astype(BF16)
        tail = jnp.concatenate([three_rows(rows), pad], axis=1)
        ref[2 * BLK :] = jnp.concatenate([tail, jnp.zeros_like(tail)], axis=0).astype(BF16)

    def low(ref):
        payload(ref, back[:BLK], part[:BLK], rows_low)

    def high(ref):
        payload(ref, back[(qb - 1) * BLK :], part[(nb - 1) * BLK :], rows_high)

    @pl.when(par == 0)
    def _():
        high(paya_ref)
        low(payb_ref)

    @pl.when(par != 0)
    def _():
        low(paya_ref)
        high(payb_ref)


def last_kernel(
    nb, heads, hdim,
    me_ref, gam_ref, _, ext_ref, gains_ref, paya_ref, payb_ref, part_ref, halo_ref, g1_ref,
    o_ref, rl_ref, v_ref, x1_ref, gd_ref, e_ref, wo, wu, wd,
    f_ref,
    datt_ref, sum_ref, ends_ref,
):
    qb = nb + 2
    par = lax.rem(me_ref[0], 2)
    ext = ext_ref[...]
    ext_t = ext.T
    from_low, _, from_high = arrange(par, None, paya_ref[...], payb_ref[...])
    from_low = from_low.astype(F32)
    from_high = from_high.astype(F32)
    part = part_ref[...]
    pieces = [halo_ref[:BLK] + from_low[BLK : 2 * BLK]]
    own_parts = [part[i * BLK : (i + 1) * BLK] for i in range(nb)]
    own_parts[0] = own_parts[0] + from_low[:BLK]
    own_parts[-1] = own_parts[-1] + from_high[:BLK]
    pieces += own_parts
    pieces.append(halo_ref[BLK:] + from_high[BLK : 2 * BLK])
    grad = jnp.concatenate(pieces, axis=0)
    du = mm_nt(grad.astype(BF16), wd[...]).astype(BF16).astype(F32)
    dinner = mm_nt((du * gd_ref[...].astype(F32)).astype(BF16), wu[...]).astype(BF16).astype(F32)
    grad = grad + rms_back(x1_ref[...], gains_ref[0, 1:2], dinner)
    datt_ref[...] = mm_nt(grad.astype(BF16), wo[...]).astype(BF16).astype(F32)

    per = LANES // hdim
    groups = heads // per
    masks = head_masks(BLK, per, hdim)
    masks2 = head_masks(2 * BLK, per, hdim)

    def cotangents(rows, g):
        cols = group_at(g)
        lane = lax.broadcasted_iota(jnp.int32, (1, LANES), 1) // hdim
        gam = jnp.zeros((1, LANES), F32)
        for h in range(per):
            gam = jnp.where(lane == h, gam_ref[0, g * per + h], gam)
        d_o = datt_ref[rows, cols] * rl_ref[rows, cols] * gam
        return d_o.astype(BF16), delta_of(d_o * o_ref[rows, cols].astype(F32), per, hdim)

    last = qb - 1
    sum_ref[...] = g1_ref[...]
    ends_ref[...] = jnp.zeros_like(ends_ref)

    def body(i, g):
        d_o, delta = cotangents(blocks_at(i + 1, 2), g)
        prods, _ = pair_products(d_o, v_ref[blocks_at(i + 1, 4), group_at(g)], masks2, per)
        for t in range(2):
            at = slice(t * BLK, (t + 1) * BLK)
            for n, c in enumerate(window_parts(t)):
                total = sum_ref[i + t, :, c]
                for h in range(per):
                    total = total + e_ref[i + t + 1, g * per + h, :, c].astype(F32) * (prods[t][h][n] - delta[h][at])
                sum_ref[i + t, :, c] = total

    def ends(_, g):
        cols = group_at(g)
        low_o, low_delta = cotangents(slice(0, BLK), g)
        high_o, high_delta = cotangents(slice(last * BLK, qb * BLK), g)
        both = jnp.concatenate([low_o, high_o], axis=1)
        both = jnp.concatenate([both * jnp.concatenate([m, m], axis=1) for m in masks], axis=0)
        prods = mm_nt(both, beside(v_ref[2 * BLK : 3 * BLK, cols], v_ref[last * BLK : qb * BLK, cols]))
        low_sum, high_sum = ends_ref[0], ends_ref[1]
        for h in range(per):
            low = prods[h * BLK : (h + 1) * BLK, :BLK] - low_delta[h]
            high = prods[h * BLK : (h + 1) * BLK, BLK:] - high_delta[h]
            low_sum = low_sum + e_ref[0, g * per + h, :, 2 * BLK :].astype(F32) * low
            high_sum = high_sum + e_ref[last, g * per + h, :, :BLK].astype(F32) * high
        ends_ref[0] = low_sum
        ends_ref[1] = high_sum

    over(nb // 2, groups, body)
    over(1, groups, ends)
    forces = [jnp.zeros((8, LANES), F32) for _ in range(nb)]
    forces[0] = forces[0] + from_low[2 * BLK : 2 * BLK + 8, :LANES]
    forces[-1] = forces[-1] + from_high[2 * BLK : 2 * BLK + 8, :LANES]
    for i in range(nb):
        total = sum_ref[i]
        sums = None
        for s in range(3):
            cols, rows = fold(total[:, s * BLK : (s + 1) * BLK], ext, ext_t, i + 2, i + 1 + s)
            sums = cols if sums is None else [a + b for a, b in zip(sums, cols)]
            j = i - 1 + s
            if 0 <= j < nb:
                forces[j] = forces[j] + three_rows(rows)
        forces[i] = forces[i] + columns_to_rows(sums)
    _, rows = fold(ends_ref[0], ext, ext_t, 1, 2)
    forces[0] = forces[0] + three_rows(rows)
    _, rows = fold(ends_ref[1], ext, ext_t, nb + 2, nb + 1)
    forces[-1] = forces[-1] + three_rows(rows)
    f_ref[...] = jnp.concatenate(forces, axis=1)[:3]


def swap_a(x):
    n = lax.axis_size("chain")
    return lax.ppermute(x, "chain", [(i, i ^ 1) for i in range(n)])


def swap_b(x):
    n = lax.axis_size("chain")
    return lax.ppermute(x, "chain", [(i, ((i + 1) ^ 1) - 1) for i in range(1, n - 1)])


def hop(x, step):
    return lax.ppermute(x, "chain", [(i, i ^ step) for i in range(lax.axis_size("chain"))])


def local(
    species, positions, block_list, embed, w_query, w_key, w_value, w_out, w_up, w_down, norm_gains, gammas, out_gain, readout
):
    atoms = species.shape[0]
    nb = atoms // BLK
    width = embed.shape[1]
    layers, heads = gammas.shape
    hdim = width // heads
    ff = w_up.shape[2]
    qb, kb = nb + 2, nb + 4
    count = lax.axis_size("chain")
    assert nb >= 2 and layers == 2 and LANES % hdim == 0 and nb % 2 == 0 and count >= 8 and count & (count - 1) == 0
    me = lax.axis_index("chain").astype(jnp.int32)
    vm = pltpu.VMEM
    smem = pl.BlockSpec(memory_space=pltpu.SMEM)

    def work(products):
        return pl.CostEstimate(flops=products * atoms * width * width * 8, transcendentals=0, bytes_accessed=0)

    vmem = pl.BlockSpec(memory_space=vm)
    keep = functools.partial(pltpu.with_memory_space_constraint, memory_space=vm)
    place = me.reshape(1)
    own = pl.pallas_call(
        functools.partial(pack_kernel, nb),
        out_shape=vm((8, atoms), F32),
        in_specs=[smem, smem, vmem, vmem],
        out_specs=vmem,
    )(place, block_list, positions, species.reshape(1, atoms))
    edge = 2 * BLK
    if atoms == edge:
        send_a = send_b = own
    else:
        first, last = own[:, :edge], own[:, -edge:]
        send_a = jnp.where(me % 2 == 0, last, first)
        send_b = jnp.where(me % 2 == 0, first, last)
    near_a, near_b = swap_a(send_a), swap_b(send_b)
    pin = functools.partial(pltpu.with_memory_space_constraint, memory_space=pltpu.HBM)
    weights = (w_query, w_key, w_value, w_out, w_up, w_down)
    shapes = [vm((width, width), BF16)] * 4 + [vm((width, ff), BF16), vm((ff, width), BF16)]
    first = pl.pallas_call(
        functools.partial(first_kernel, nb, heads, hdim),
        out_shape=[
            vm((8, LANES), F32), vm((8, kb * BLK), F32), vm(norm_gains.shape, F32),
            vm((qb * BLK, width), BF16), vm((qb * BLK, width), F32), vm((kb * BLK, width), BF16),
            vm((qb * BLK, width), F32), vm((qb * BLK, ff), BF16), vm((qb, heads, BLK, 3 * BLK), BF16), *shapes[3:],
            vm((qb * BLK, width), F32), vm((nb * BLK, width), BF16), vm((qb * BLK, width), BF16),
            vm((qb * BLK, width), BF16), vm((nb * BLK, width), BF16), vm((nb * BLK, width), F32),
            vm((nb, heads, BLK, 3 * BLK), BF16), vm((nb * BLK, width), F32), vm((nb * BLK, ff), BF16),
            vm((nb * BLK, width), F32), *shapes,
        ],
        in_specs=[smem, smem] + [vmem] * 7 + [pl.BlockSpec(memory_space=pltpu.HBM)] * 6,
        out_specs=[vmem] * 28,
        scratch_shapes=[
            *shapes[:3], vm((qb, BLK, 3 * BLK), F32), vm((qb * BLK, width), F32), vm((qb * BLK, width), BF16),
            vm((kb * BLK, width), BF16), vm((LANES // hdim, kb * BLK, width), BF16),
            vm((LANES // hdim, qb * BLK, width), BF16), pltpu.SemaphoreType.DMA((2, 6)),
        ],
        compiler_params=pltpu.CompilerParams(vmem_limit_bytes=20 * 1024 * 1024),
        cost_estimate=work(qb * 7),
    )(
        place, gammas, keep(own), keep(near_a), keep(near_b), pin(embed), pin(norm_gains),
        pin(out_gain.reshape(1, width)), pin(readout.reshape(1, width)), *(pin(w) for w in weights),
    )
    energy, ext, gains = first[0], keep(first[1]), keep(first[2])
    saved0 = [keep(x) for x in first[3:12]]
    saved1 = [keep(x) for x in first[12:]]
    energy = energy + hop(energy, 1)
    pay = vm((2 * BLK + 16, width), BF16)
    pay_a, pay_b, part, halo, pairs = pl.pallas_call(
        functools.partial(middle_kernel, nb, heads, hdim),
        out_shape=[pay, pay, vm((nb * BLK, width), F32), vm((2 * BLK, width), F32), vm((nb, BLK, 3 * BLK), F32)],
        in_specs=[smem, smem] + [vmem] * 19,
        out_specs=[vmem] * 5,
        scratch_shapes=[
            vm((nb * BLK, width), BF16), vm((qb * BLK, width), F32), vm((qb * BLK, width), F32), vm((nb * BLK, width), F32),
        ],
        compiler_params=pltpu.CompilerParams(vmem_limit_bytes=20 * 1024 * 1024),
        cost_estimate=work(nb * 9),
    )(place, gammas, keep(energy), ext, gains, *saved1)
    energy = energy + hop(energy, 2)
    energy, pay_a, pay_b = lax.optimization_barrier((energy, pay_a, pay_b))
    arriving = hop(energy, 4)
    got_a, got_b = swap_a(pay_a), swap_b(pay_b)
    energy = energy + arriving
    forces = pl.pallas_call(
        functools.partial(last_kernel, nb, heads, hdim),
        out_shape=jax.ShapeDtypeStruct((3, atoms), F32),
        in_specs=[smem, smem] + [vmem] * 17,
        out_specs=vmem,
        scratch_shapes=[vm((qb * BLK, width), F32), vm((nb, BLK, 3 * BLK), F32), vm((2, BLK, BLK), F32)],
        compiler_params=pltpu.CompilerParams(vmem_limit_bytes=20 * 1024 * 1024),
        cost_estimate=work(qb * 3),
    )(
        place, gammas, keep(energy), ext, gains, keep(got_a), keep(got_b), keep(part), keep(halo), keep(pairs), *saved0
    )
    if count > 8:
        arriving = hop(energy, 8)
        energy, forces = lax.optimization_barrier((energy, forces))
        energy = energy + arriving
    step = 16
    while step < count:
        energy = energy + hop(energy, step)
        step *= 2
    return energy[:1, :1].reshape(1), forces


def solution(mesh):
    sharded = ("frames", "chain")
    return jax.shard_map(
        local,
        mesh=mesh,
        in_specs=(P(sharded), P(None, sharded), P(sharded, None)) + (P(),) * 11,
        out_specs=(P("frames"), P(None, sharded)),
        check_vma=False,
    )
```

```python
import functools
import math

import jax
import jax.numpy as jnp
from jax import lax
from jax.experimental import pallas as pl
from jax.experimental.pallas import tpu as pltpu
from jax.sharding import PartitionSpec as P

BLK = 128
LANES = 128
EPS = 1e-06
FAR = 1e30
F32 = jnp.float32
BF16 = jnp.bfloat16
C0 = math.sqrt(2.0 / math.pi)
C1 = 0.044715


def mm(a, b):
    return jnp.dot(a, b, preferred_element_type=F32)


def mm_nt(a, b):
    return lax.dot_general(a, b, (((1,), (1,)), ((), ())), preferred_element_type=F32)


def mm_tn(a, b):
    return lax.dot_general(a, b, (((0,), (0,)), ((), ())), preferred_element_type=F32)


def inv_rms(x):
    return lax.rsqrt(jnp.mean(x * x, axis=-1, keepdims=True) + EPS)


def rms_back(x, gain, cot):
    r = inv_rms(x)
    t = cot * gain
    return r * (t - x * (r * r * jnp.mean(x * t, axis=-1, keepdims=True)))


def gelu_half(x):
    return 0.5 + 0.5 * jnp.tanh(x * (C0 + (C0 * C1) * (x * x)))


def gelu_slope(x):
    half = gelu_half(x)
    return half + (x * half) * (1.0 - half) * (2.0 * C0 + (6.0 * C0 * C1) * (x * x))


def head_masks(rows, heads_per_group, hdim):
    lane = lax.broadcasted_iota(jnp.int32, (rows, LANES), 1) // hdim
    return [(lane == h).astype(F32).astype(BF16) for h in range(heads_per_group)]


def arrange(par, own, from_a, from_b):
    before = jnp.where(par == 0, from_b, from_a)
    after = jnp.where(par == 0, from_a, from_b)
    return before, own, after


def distances(ext, ext_t, first, d2_ref, count):
    for i in range(count):
        q = ext_t[(first + i) * BLK : (first + i + 1) * BLK]
        for s in range(3):
            k0 = (first + i - 1 + s) * BLK
            tot = None
            for c in range(3):
                diff = q[:, c : c + 1] - ext[c : c + 1, k0 : k0 + BLK]
                tot = diff * diff if tot is None else tot + diff * diff
            listed = ext[4 + s : 5 + s, (first + i) * BLK : (first + i + 1) * BLK] > 0.5
            d2_ref[i, :, s * BLK : (s + 1) * BLK] = jnp.where(listed, tot, FAR)


def stacked(x, masks):
    return jnp.concatenate([x * m for m in masks], axis=0)


def beside(x, y):
    zero = jnp.zeros_like(x)
    return jnp.concatenate([jnp.concatenate([x, zero], axis=1), jnp.concatenate([zero, y], axis=1)], axis=0)


def pair_products(a, b, masks2, per):
    each = [a * m for m in masks2]
    shared = mm_nt(jnp.concatenate(each, axis=0), b[BLK : 3 * BLK])
    both = jnp.concatenate([jnp.concatenate([x[:BLK], x[BLK:]], axis=1) for x in each], axis=0)
    outer = mm_nt(both, beside(b[:BLK], b[3 * BLK :]))
    got = []
    for t in range(2):
        got.append([
            (outer[h * BLK : (h + 1) * BLK, t * BLK : (t + 1) * BLK], shared[(2 * h + t) * BLK : (2 * h + t + 1) * BLK])
            for h in range(per)
        ])
    return got, each


def span(first, size, unit):
    if isinstance(first, int):
        return slice(first * unit, first * unit + size)
    return pl.ds(pl.multiple_of(first * unit, unit), size)


def blocks_at(first, count):
    return span(first, count * BLK, BLK)


def group_at(g):
    return span(g, LANES, LANES)


def over(pairs, groups, body, rolled=False):
    if rolled:
        lax.fori_loop(0, pairs * groups, lambda n, _: (body(2 * lax.div(n, groups), lax.rem(n, groups)), 0)[1], 0)
    else:
        for n in range(pairs * groups):
            body(2 * (n // groups), n % groups)


def window_parts(t):
    return (slice(0, BLK), slice(BLK, 3 * BLK)) if t == 0 else (slice(2 * BLK, 3 * BLK), slice(0, 2 * BLK))


def head_norms(x, hdim):
    width = x.shape[1]
    lane = lax.broadcasted_iota(jnp.int32, (width, LANES), 0) // hdim
    member = (lane == lax.broadcasted_iota(jnp.int32, (width, LANES), 1)).astype(F32).astype(BF16)
    x = x.astype(F32)
    return jnp.max(mm((x * x).astype(BF16), member), axis=0, keepdims=True)


def small_scores(q, k, hdim):
    return jnp.max(head_norms(q, hdim) * head_norms(k, hdim)) < 1600.0 * hdim


def attend(exact, q_ref, k_ref, vm_ref, o_ref, rl_ref, e_ref, d2_ref, d2_first, gam_ref, layer, heads, hdim, count):
    per = LANES // hdim
    groups = heads // per
    scale = hdim ** (-0.5)
    masks2 = head_masks(2 * BLK, per, hdim)
    ones2 = jnp.concatenate(masks2, axis=0)
    ones1 = jnp.concatenate([m[:BLK] for m in masks2], axis=0)

    def values(first, blocks, cols, ones):
        rows = blocks_at(first, blocks)
        return jnp.concatenate([jnp.concatenate([vm_ref[h, rows, cols] for h in range(per)], axis=0), ones], axis=1)

    def body(i, g):
        cols = group_at(g)
        scores, _ = pair_products(q_ref[blocks_at(i, 2), cols], k_ref[blocks_at(i, 4), cols], masks2, per)
        sides, middles = [], []
        for t in range(2):
            outer_cols, shared_cols = window_parts(t)
            outers, shareds = [], []
            for h in range(per):
                gam = gam_ref[layer, g * per + h] / scale
                outer, shared = scores[t][h]
                outer = outer - gam * d2_ref[d2_first + i + t, :, outer_cols]
                shared = shared - gam * d2_ref[d2_first + i + t, :, shared_cols]
                if exact:
                    peak = jnp.maximum(jnp.maximum(outer, shared[:, :BLK]), shared[:, BLK:])
                    peak = jnp.max(peak, axis=1, keepdims=True)
                    outer, shared = outer - peak, shared - peak
                outer = jnp.exp(outer * scale).astype(BF16)
                shared = jnp.exp(shared * scale).astype(BF16)
                e_ref[i + t, g * per + h, :, outer_cols] = outer
                e_ref[i + t, g * per + h, :, shared_cols] = shared
                outers.append(outer)
                shareds.append(shared)
            middles.append(jnp.concatenate(shareds, axis=1))
            sides.append(mm(jnp.concatenate(outers, axis=1), values(i + 3 * t, 1, cols, ones1)))
        out = mm(jnp.concatenate(middles, axis=0), values(i + 1, 2, cols, ones2)) + jnp.concatenate(sides, axis=0)
        rl = 1.0 / jnp.maximum(out[:, LANES:], 1e-37)
        rl_ref[blocks_at(i, 2), cols] = rl
        o_ref[blocks_at(i, 2), cols] = (out[:, :LANES] * rl).astype(BF16)

    over(count // 2, groups, body, rolled=exact)


def split_heads(v_ref, vm_ref, hdim):
    rows, width = v_ref.shape
    masks = head_masks(BLK, LANES // hdim, hdim)
    for r in range(0, rows, BLK):
        for c in range(0, width, LANES):
            for h, m in enumerate(masks):
                vm_ref[h, r : r + BLK, c : c + LANES] = v_ref[r : r + BLK, c : c + LANES] * m


def delta_of(prod, per, hdim):
    lane = lax.broadcasted_iota(jnp.int32, prod.shape, 1) // hdim
    return [jnp.sum(jnp.where(lane == h, prod, 0.0), axis=1, keepdims=True) for h in range(per)]


def fold(grad, ext, ext_t, qb, kb):
    cols, rows = [], []
    for c in range(3):
        diff = ext_t[qb * BLK : (qb + 1) * BLK, c : c + 1] - ext[c : c + 1, kb * BLK : (kb + 1) * BLK]
        t = grad * diff
        cols.append(2.0 * jnp.sum(t, axis=1, keepdims=True))
        rows.append(-2.0 * jnp.sum(t, axis=0, keepdims=True))
    return cols, rows


def columns_to_rows(cols):
    lane = lax.broadcasted_iota(jnp.int32, (BLK, LANES), 1)
    wide = jnp.zeros((BLK, LANES), F32)
    for c in range(3):
        wide = jnp.where(lane == c, cols[c], wide)
    return wide.T[:8]


def three_rows(rows):
    sub = lax.broadcasted_iota(jnp.int32, (8, LANES), 0)
    out = jnp.zeros((8, LANES), F32)
    for c in range(3):
        out = jnp.where(sub == c, rows[c], out)
    return out


def pack_kernel(nb, me_ref, list_ref, pos_ref, spec_ref, own_ref):
    own_ref[...] = jnp.zeros_like(own_ref)
    own_ref[0:3] = pos_ref[...]
    own_ref[3:4] = spec_ref[...].astype(F32)
    for b in range(nb):
        for s in range(3):
            listed = list_ref[b, s]
            ok = jnp.logical_and(listed == me_ref[0] * nb + (b - 1 + s), listed >= 0)
            own_ref[4 + s : 5 + s, b * BLK : (b + 1) * BLK] = jnp.full((1, BLK), ok.astype(F32))


def first_kernel(
    nb, heads, hdim,
    me_ref, gam_ref, gamv_ref, own_ref, ra_ref, rb_ref, embed_ref, gains_ref, outg_ref, ro_ref,
    wq_h, wk_h, wv_h, wo_h, wu_h, wd_h,
    e_out, ext_ref, gk_ref, gamk_ref, par_out, o_ref, rl_ref, v_ref, x1_ref, gd_ref, e_ref, wo0, wu0, wd0,
    st_ref, q1_ref, k1_ref, v1_ref, o1_ref, rl1_ref, e1_ref, x11_ref, gd1_ref, top_ref, wq1, wk1, wv1, wo1, wu1, wd1,
    wq0, wk0, wv0, d2_ref, x0_ref, q_ref, k_ref, vm_ref, vm1_ref, sem,
):
    qb = nb + 2
    kb = nb + 4
    mid = slice(BLK, (nb + 1) * BLK)
    sources = (wq_h, wk_h, wv_h, wo_h, wu_h, wd_h)
    targets = ((wq0, wk0, wv0, wo0, wu0, wd0), (wq1, wk1, wv1, wo1, wu1, wd1))
    copies = []
    for layer in range(2):
        copies.append([
            pltpu.make_async_copy(src.at[layer], dst, sem.at[layer, n])
            for n, (src, dst) in enumerate(zip(sources, targets[layer]))
        ])
        for c in copies[layer]:
            c.start()
    par = lax.rem(me_ref[0], 2)
    before, own, after = arrange(par, own_ref[...], ra_ref[...], rb_ref[...])
    ext = jnp.concatenate([before, own, after], axis=1)
    ext_ref[...] = ext
    gk_ref[...] = gains_ref[...]
    par_out[...] = jnp.full(par_out.shape, par.astype(F32))
    rates = gamv_ref[...].T
    for layer in range(2):
        gamk_ref[layer] = jnp.broadcast_to(rates[:, layer : layer + 1], (heads, LANES))
    ext_t = ext.T
    distances(ext, ext_t, 1, d2_ref, qb)

    embed = embed_ref[...].astype(F32)
    normed = (embed * inv_rms(embed) * gains_ref[0, 0:1]).astype(BF16)
    scale = hdim ** (-0.5)
    spec = ext_t[:, 3:4].astype(jnp.int32)
    nspec = embed_ref.shape[0]
    onehot = (spec == lax.broadcasted_iota(jnp.int32, (kb * BLK, nspec), 1)).astype(F32).astype(BF16)
    onehot_q = onehot[BLK : (qb + 1) * BLK]
    x0_ref[...] = mm(onehot_q, embed_ref[...])
    for c in copies[0][:3]:
        c.wait()
    q_table = mm(normed, wq0[...]).astype(BF16)
    q_ref[...] = mm(onehot_q, q_table).astype(BF16)
    k_table = mm(normed, wk0[...]).astype(BF16)
    k_ref[...] = mm(onehot, k_table).astype(BF16)
    v_ref[...] = mm(onehot, mm(normed, wv0[...]).astype(BF16)).astype(BF16)
    split_heads(v_ref, vm_ref, hdim)

    def run(exact):
        def arrived(some):
            if not exact:
                for c in some:
                    c.wait()

        attend(exact, q_ref, k_ref, vm_ref, o_ref, rl_ref, e_ref, d2_ref, 0, gam_ref, 0, heads, hdim, qb)

        arrived(copies[0][3:])

        def feed(layer, x1, w_up, w_down, keep):
            inner = (x1 * inv_rms(x1) * gains_ref[layer, 1:2]).astype(BF16)
            pre = mm(inner, w_up[...])
            keep(pre)
            return x1 + mm((pre * gelu_half(pre)).astype(BF16), w_down[...])

        step = 4 * BLK
        for r in range(0, qb * BLK, step):
            rows = slice(r, r + step)
            x1 = x0_ref[rows] + mm(o_ref[rows], wo0[...])
            x1_ref[rows] = x1
            st_ref[rows] = feed(0, x1, wu0, wd0, lambda pre: gd_ref.__setitem__(rows, pre))

        arrived(copies[1])
        gain = gains_ref[1, 0:1]
        st = st_ref[...]
        normed = (st * inv_rms(st) * gain).astype(BF16)
        q1_ref[...] = mm(normed[mid], wq1[...]).astype(BF16)
        k1_ref[...] = mm(normed, wk1[...]).astype(BF16)
        v1_ref[...] = mm(normed, wv1[...]).astype(BF16)
        split_heads(v1_ref, vm1_ref, hdim)
        attend(exact, q1_ref, k1_ref, vm1_ref, o1_ref, rl1_ref, e1_ref, d2_ref, 1, gam_ref, 1, heads, hdim, nb)
        x1 = st_ref[mid] + mm(o1_ref[...], wo1[...])
        x11_ref[...] = x1
        x2 = feed(1, x1, wu1, wd1, lambda pre: gd1_ref.__setitem__(..., pre))

        w = outg_ref[...] * ro_ref[...]
        r = inv_rms(x2)
        along = jnp.sum(x2 * w, axis=1, keepdims=True)
        e_out[...] = jnp.broadcast_to(jnp.sum(along * r), e_out.shape)
        width = x2.shape[1]
        top_ref[...] = r * (w - x2 * (r * r * along * (1.0 / width)))

    run(False)
    small = jnp.logical_and(small_scores(q_table, k_table, hdim), small_scores(q1_ref[...], k1_ref[...], hdim))

    @pl.when(jnp.logical_not(small))
    def _():
        run(True)


def middle_kernel(
    nb, heads, hdim,
    par_ref, gam_ref, _, ext_ref, gains_ref, st_ref, q1_ref, k1_ref, v1_ref, o1_ref, rl1_ref, e1_ref, x1_ref, gd_ref, top_ref,
    wq, wk, wv, wo, wu, wd,
    paya_ref, payb_ref, part_ref, halo_ref, g1_ref,
    dq_ref, dk_ref, dv_ref, datt_ref,
):
    qb = nb + 2
    mid = slice(BLK, (nb + 1) * BLK)
    scale = hdim ** (-0.5)
    width = st_ref.shape[1]
    even = par_ref[0:1, 0:1] < 0.5
    ext = ext_ref[...]
    ext_t = ext.T
    grad = top_ref[...]
    du = mm_nt(grad.astype(BF16), wd[...]).astype(BF16).astype(F32)
    dinner = mm_nt((du * gelu_slope(gd_ref[...])).astype(BF16), wu[...]).astype(BF16).astype(F32)
    grad = grad + rms_back(x1_ref[...], gains_ref[1, 1:2], dinner)
    datt_ref[...] = mm_nt(grad.astype(BF16), wo[...]).astype(BF16).astype(F32)

    per = LANES // hdim
    groups = heads // per
    masks2 = head_masks(2 * BLK, per, hdim)
    masks3 = head_masks(3 * BLK, per, hdim)
    dk_ref[...] = jnp.zeros_like(dk_ref)
    dv_ref[...] = jnp.zeros_like(dv_ref)
    g1_ref[...] = jnp.zeros_like(g1_ref)

    def body(i, g):
        cols = group_at(g)
        rows2 = blocks_at(i, 2)
        d_o = datt_ref[rows2, cols] * rl1_ref[rows2, cols]
        delta = delta_of(d_o * o1_ref[rows2, cols].astype(F32), per, hdim)
        prods, each_do = pair_products(d_o.astype(BF16), v1_ref[blocks_at(i, 4), cols], masks2, per)
        q = q1_ref[rows2, cols]
        each_q = [q * m for m in masks2]
        es, dss = [], []
        for t in range(2):
            at = slice(t * BLK, (t + 1) * BLK)
            rows, win = blocks_at(i + t, 1), blocks_at(i + t, 3)
            outer_cols, shared_cols = window_parts(t)
            parts = []
            pair_outer = g1_ref[i + t, :, outer_cols]
            pair_shared = g1_ref[i + t, :, shared_cols]
            for h in range(per):
                e_outer, e_shared = e1_ref[i + t, g * per + h, :, outer_cols], e1_ref[i + t, g * per + h, :, shared_cols]
                outer, shared = prods[t][h]
                gam = gam_ref[1, g * per + h : g * per + h + 1]
                outer = e_outer.astype(F32) * (outer - delta[h][at])
                shared = e_shared.astype(F32) * (shared - delta[h][at])
                pair_outer = pair_outer + gam * outer
                pair_shared = pair_shared + jnp.concatenate([gam, gam], axis=1) * shared
                outer, shared = outer.astype(BF16), shared.astype(BF16)
                parts.append(jnp.concatenate([outer, shared] if t == 0 else [shared, outer], axis=1))
                es.append((e_outer, e_shared))
                dss.append((outer, shared))
            g1_ref[i + t, :, outer_cols] = pair_outer
            g1_ref[i + t, :, shared_cols] = pair_shared
            ks = stacked(k1_ref[win, cols], masks3)
            dq_ref[rows, cols] = (mm(jnp.concatenate(parts, axis=1), ks) * scale).astype(BF16)
        for ref, each, weights in ((dk_ref, each_q, dss), (dv_ref, each_do, es)):
            left = jnp.concatenate([x[t * BLK : (t + 1) * BLK] for t in range(2) for x in each], axis=0).T
            ref[cols, blocks_at(i + 1, 2)] += mm(left, jnp.concatenate([w[1] for w in weights], axis=0))
            for t in range(2):
                some = slice(t * per, (t + 1) * per)
                ref[cols, blocks_at(i + 3 * t, 1)] += mm(
                    left[:, t * per * BLK : (t + 1) * per * BLK], jnp.concatenate([w[0] for w in weights[some]], axis=0)
                )

    over(nb // 2, groups, body)
    dk = (dk_ref[...] * scale).astype(BF16).T
    dv = dv_ref[...].astype(BF16).T
    dnorm = mm_nt(dk, wk[...]) + mm_nt(dv, wv[...])
    dq = mm_nt(dq_ref[...], wq[...])
    zeros = jnp.zeros((BLK, width), F32)
    dnorm = dnorm + jnp.concatenate([zeros, dq, zeros], axis=0)
    back = rms_back(st_ref[...], gains_ref[1, 0:1], dnorm.astype(BF16).astype(F32))
    part = grad + back[mid]
    part_ref[...] = part
    halo_ref[:BLK] = back[:BLK]
    halo_ref[BLK:] = back[(qb - 1) * BLK :]

    _, rows_low = fold(g1_ref[0, :, :BLK], ext, ext_t, 2, 1)
    _, rows_high = fold(g1_ref[nb - 1, :, 2 * BLK :], ext, ext_t, nb + 1, nb + 2)
    pad = jnp.zeros((8, width - LANES), F32)

    def payload(halo, edge, rows):
        tail = jnp.concatenate([three_rows(rows), pad], axis=1)
        return halo, edge, jnp.concatenate([tail, jnp.zeros_like(tail)], axis=0)

    low = payload(back[:BLK], part[:BLK], rows_low)
    high = payload(back[(qb - 1) * BLK :], part[(nb - 1) * BLK :], rows_high)
    at = 0
    for x, y in zip(high, low):
        rows = slice(at, at + x.shape[0])
        paya_ref[rows] = jnp.where(even, x, y).astype(BF16)
        payb_ref[rows] = jnp.where(even, y, x).astype(BF16)
        at += x.shape[0]


def slope_kernel(_, pre_ref, out_ref):
    out_ref[...] = gelu_slope(pre_ref[...]).astype(BF16)


def last_kernel(
    nb, heads, hdim,
    par_ref, gam_ref, _, ext_ref, gains_ref, paya_ref, payb_ref, part_ref, halo_ref, g1_ref,
    o_ref, rl_ref, v_ref, x1_ref, gd_ref, e_ref, wo, wu, wd,
    f_ref,
    datt_ref, sum_ref, ends_ref,
):
    qb = nb + 2
    ext = ext_ref[...]
    ext_t = ext.T
    even = par_ref[0:1, 0:1] < 0.5
    from_a, from_b = paya_ref[...].astype(F32), payb_ref[...].astype(F32)
    from_low, from_high = jnp.where(even, from_b, from_a), jnp.where(even, from_a, from_b)
    part = part_ref[...]
    pieces = [halo_ref[:BLK] + from_low[BLK : 2 * BLK]]
    own_parts = [part[i * BLK : (i + 1) * BLK] for i in range(nb)]
    own_parts[0] = own_parts[0] + from_low[:BLK]
    own_parts[-1] = own_parts[-1] + from_high[:BLK]
    pieces += own_parts
    pieces.append(halo_ref[BLK:] + from_high[BLK : 2 * BLK])
    grad = jnp.concatenate(pieces, axis=0)
    du = mm_nt(grad.astype(BF16), wd[...]).astype(BF16).astype(F32)
    dinner = mm_nt((du * gd_ref[...].astype(F32)).astype(BF16), wu[...]).astype(BF16).astype(F32)
    grad = grad + rms_back(x1_ref[...], gains_ref[0, 1:2], dinner)
    datt_ref[...] = mm_nt(grad.astype(BF16), wo[...]).astype(BF16).astype(F32)

    per = LANES // hdim
    groups = heads // per
    masks = head_masks(BLK, per, hdim)
    masks2 = head_masks(2 * BLK, per, hdim)

    def cotangents(rows, g):
        cols = group_at(g)
        lane = lax.broadcasted_iota(jnp.int32, (1, LANES), 1) // hdim
        gam = jnp.zeros((1, LANES), F32)
        for h in range(per):
            gam = jnp.where(lane == h, gam_ref[0, g * per + h : g * per + h + 1], gam)
        d_o = datt_ref[rows, cols] * rl_ref[rows, cols] * gam
        return d_o.astype(BF16), delta_of(d_o * o_ref[rows, cols].astype(F32), per, hdim)

    last = qb - 1
    sum_ref[...] = g1_ref[...]
    ends_ref[...] = jnp.zeros_like(ends_ref)

    def body(i, g):
        d_o, delta = cotangents(blocks_at(i + 1, 2), g)
        prods, _ = pair_products(d_o, v_ref[blocks_at(i + 1, 4), group_at(g)], masks2, per)
        for t in range(2):
            at = slice(t * BLK, (t + 1) * BLK)
            for n, c in enumerate(window_parts(t)):
                total = sum_ref[i + t, :, c]
                for h in range(per):
                    total = total + e_ref[i + t + 1, g * per + h, :, c].astype(F32) * (prods[t][h][n] - delta[h][at])
                sum_ref[i + t, :, c] = total

    def ends(_, g):
        cols = group_at(g)
        low_o, low_delta = cotangents(slice(0, BLK), g)
        high_o, high_delta = cotangents(slice(last * BLK, qb * BLK), g)
        both = jnp.concatenate([low_o, high_o], axis=1)
        both = jnp.concatenate([both * jnp.concatenate([m, m], axis=1) for m in masks], axis=0)
        prods = mm_nt(both, beside(v_ref[2 * BLK : 3 * BLK, cols], v_ref[last * BLK : qb * BLK, cols]))
        low_sum, high_sum = ends_ref[0], ends_ref[1]
        for h in range(per):
            low = prods[h * BLK : (h + 1) * BLK, :BLK] - low_delta[h]
            high = prods[h * BLK : (h + 1) * BLK, BLK:] - high_delta[h]
            low_sum = low_sum + e_ref[0, g * per + h, :, 2 * BLK :].astype(F32) * low
            high_sum = high_sum + e_ref[last, g * per + h, :, :BLK].astype(F32) * high
        ends_ref[0] = low_sum
        ends_ref[1] = high_sum

    over(nb // 2, groups, body)
    over(1, groups, ends)
    forces = [jnp.zeros((8, LANES), F32) for _ in range(nb)]
    forces[0] = forces[0] + from_low[2 * BLK : 2 * BLK + 8, :LANES]
    forces[-1] = forces[-1] + from_high[2 * BLK : 2 * BLK + 8, :LANES]
    for i in range(nb):
        total = sum_ref[i]
        sums = None
        for s in range(3):
            cols, rows = fold(total[:, s * BLK : (s + 1) * BLK], ext, ext_t, i + 2, i + 1 + s)
            sums = cols if sums is None else [a + b for a, b in zip(sums, cols)]
            j = i - 1 + s
            if 0 <= j < nb:
                forces[j] = forces[j] + three_rows(rows)
        forces[i] = forces[i] + columns_to_rows(sums)
    _, rows = fold(ends_ref[0], ext, ext_t, 1, 2)
    forces[0] = forces[0] + three_rows(rows)
    _, rows = fold(ends_ref[1], ext, ext_t, nb + 2, nb + 1)
    forces[-1] = forces[-1] + three_rows(rows)
    f_ref[...] = jnp.concatenate(forces, axis=1)[:3]


def swap_a(x):
    n = lax.axis_size("chain")
    return lax.ppermute(x, "chain", [(i, i ^ 1) for i in range(n)])


def swap_b(x):
    n = lax.axis_size("chain")
    return lax.ppermute(x, "chain", [(i, ((i + 1) ^ 1) - 1) for i in range(1, n - 1)])


def hop(x, step):
    return lax.ppermute(x, "chain", [(i, i ^ step) for i in range(lax.axis_size("chain"))])


def local(
    species, positions, block_list, embed, w_query, w_key, w_value, w_out, w_up, w_down, norm_gains, gammas, out_gain, readout
):
    atoms = species.shape[0]
    nb = atoms // BLK
    width = embed.shape[1]
    layers, heads = gammas.shape
    hdim = width // heads
    ff = w_up.shape[2]
    qb, kb = nb + 2, nb + 4
    count = lax.axis_size("chain")
    assert nb >= 2 and layers == 2 and LANES % hdim == 0 and nb % 2 == 0 and count >= 8 and count & (count - 1) == 0
    me = lax.axis_index("chain").astype(jnp.int32)
    vm = pltpu.VMEM
    smem = pl.BlockSpec(memory_space=pltpu.SMEM)

    def work(products):
        return pl.CostEstimate(flops=products * atoms * width * width * 8, transcendentals=0, bytes_accessed=0)

    vmem = pl.BlockSpec(memory_space=vm)
    keep = functools.partial(pltpu.with_memory_space_constraint, memory_space=vm)
    place = me.reshape(1)
    own = pl.pallas_call(
        functools.partial(pack_kernel, nb),
        out_shape=vm((8, atoms), F32),
        in_specs=[smem, smem, vmem, vmem],
        out_specs=vmem,
    )(place, block_list, positions, species.reshape(1, atoms))
    edge = 2 * BLK
    if atoms == edge:
        send_a = send_b = own
    else:
        first, last = own[:, :edge], own[:, -edge:]
        send_a = jnp.where(me % 2 == 0, last, first)
        send_b = jnp.where(me % 2 == 0, first, last)
    near_a, near_b = swap_a(send_a), swap_b(send_b)
    pin = functools.partial(pltpu.with_memory_space_constraint, memory_space=pltpu.HBM)
    gammas = pin(gammas)
    weights = (w_query, w_key, w_value, w_out, w_up, w_down)
    shapes = [vm((width, width), BF16)] * 4 + [vm((width, ff), BF16), vm((ff, width), BF16)]
    first = pl.pallas_call(
        functools.partial(first_kernel, nb, heads, hdim),
        out_shape=[
            vm((8, LANES), F32), vm((8, kb * BLK), F32), vm(norm_gains.shape, F32),
            vm((layers, heads, LANES), F32), vm((8, LANES), F32),
            vm((qb * BLK, width), BF16), vm((qb * BLK, width), F32), vm((kb * BLK, width), BF16),
            vm((qb * BLK, width), F32), vm((qb * BLK, ff), F32), vm((qb, heads, BLK, 3 * BLK), BF16), *shapes[3:],
            vm((qb * BLK, width), F32), vm((nb * BLK, width), BF16), vm((qb * BLK, width), BF16),
            vm((qb * BLK, width), BF16), vm((nb * BLK, width), BF16), vm((nb * BLK, width), F32),
            vm((nb, heads, BLK, 3 * BLK), BF16), vm((nb * BLK, width), F32), vm((nb * BLK, ff), F32),
            vm((nb * BLK, width), F32), *shapes,
        ],
        in_specs=[smem, smem] + [vmem] * 8 + [pl.BlockSpec(memory_space=pltpu.HBM)] * 6,
        out_specs=[vmem] * 30,
        scratch_shapes=[
            *shapes[:3], vm((qb, BLK, 3 * BLK), F32), vm((qb * BLK, width), F32), vm((qb * BLK, width), BF16),
            vm((kb * BLK, width), BF16), vm((LANES // hdim, kb * BLK, width), BF16),
            vm((LANES // hdim, qb * BLK, width), BF16), pltpu.SemaphoreType.DMA((2, 6)),
        ],
        compiler_params=pltpu.CompilerParams(vmem_limit_bytes=20 * 1024 * 1024),
        cost_estimate=work(qb * 7),
    )(
        place, gammas, gammas, keep(own), keep(near_a), keep(near_b), pin(embed), pin(norm_gains),
        pin(out_gain.reshape(1, width)), pin(readout.reshape(1, width)), *(pin(w) for w in weights),
    )
    energy, ext, gains = first[0], keep(first[1]), keep(first[2])
    rates, side = keep(first[3]), keep(first[4])
    saved0 = [keep(x) for x in first[5:14]]
    saved1 = [keep(x) for x in first[14:]]
    energy = energy + hop(energy, 1)
    pay = vm((2 * BLK + 16, width), BF16)
    pay_a, pay_b, part, halo, pairs = pl.pallas_call(
        functools.partial(middle_kernel, nb, heads, hdim),
        out_shape=[pay, pay, vm((nb * BLK, width), F32), vm((2 * BLK, width), F32), vm((nb, BLK, 3 * BLK), F32)],
        in_specs=[vmem] * 21,
        out_specs=[vmem] * 5,
        scratch_shapes=[
            vm((nb * BLK, width), BF16), vm((width, qb * BLK), F32), vm((width, qb * BLK), F32), vm((nb * BLK, width), F32),
        ],
        compiler_params=pltpu.CompilerParams(vmem_limit_bytes=20 * 1024 * 1024),
        cost_estimate=work(nb * 9),
    )(side, rates, keep(energy), ext, gains, *saved1)
    energy = energy + hop(energy, 2)
    energy, pay_a, pay_b = lax.optimization_barrier((energy, pay_a, pay_b))
    saved0[4] = keep(
        pl.pallas_call(
            slope_kernel,
            out_shape=vm((qb * BLK, ff), BF16),
            in_specs=[vmem, vmem],
            out_specs=vmem,
            compiler_params=pltpu.CompilerParams(vmem_limit_bytes=8 * 1024 * 1024),
            cost_estimate=work(qb),
        )(keep(energy), saved0[4])
    )
    arriving = hop(energy, 4)
    got_a, got_b = swap_a(pay_a), swap_b(pay_b)
    energy = energy + arriving
    forces = pl.pallas_call(
        functools.partial(last_kernel, nb, heads, hdim),
        out_shape=jax.ShapeDtypeStruct((3, atoms), F32),
        in_specs=[vmem] * 19,
        out_specs=vmem,
        scratch_shapes=[vm((qb * BLK, width), F32), vm((nb, BLK, 3 * BLK), F32), vm((2, BLK, BLK), F32)],
        compiler_params=pltpu.CompilerParams(vmem_limit_bytes=20 * 1024 * 1024),
        cost_estimate=work(qb * 3),
    )(
        side, rates, keep(energy), ext, gains, keep(got_a), keep(got_b), keep(part), keep(halo), keep(pairs), *saved0
    )
    if count > 8:
        arriving = hop(energy, 8)
        energy, forces = lax.optimization_barrier((energy, forces))
        energy = energy + arriving
    step = 16
    while step < count:
        energy = energy + hop(energy, step)
        step *= 2
    return energy[:1, :1].reshape(1), forces


def solution(mesh):
    sharded = ("frames", "chain")
    return jax.shard_map(
        local,
        mesh=mesh,
        in_specs=(P(sharded), P(None, sharded), P(sharded, None)) + (P(),) * 11,
        out_specs=(P("frames"), P(None, sharded)),
        check_vma=False,
    )
```

```python
import functools
import math

import jax
import jax.numpy as jnp
from jax import lax
from jax.experimental import pallas as pl
from jax.experimental.pallas import tpu as pltpu
from jax.sharding import PartitionSpec as P

BLK = 128
LANES = 128
EPS = 1e-06
FAR = 1e30
F32 = jnp.float32
BF16 = jnp.bfloat16
C0 = math.sqrt(2.0 / math.pi)
C1 = 0.044715


def mm(a, b):
    return jnp.dot(a, b, preferred_element_type=F32)


def mm_nt(a, b):
    return lax.dot_general(a, b, (((1,), (1,)), ((), ())), preferred_element_type=F32)


def mm_tn(a, b):
    return lax.dot_general(a, b, (((0,), (0,)), ((), ())), preferred_element_type=F32)


def inv_rms(x):
    return lax.rsqrt(jnp.mean(x * x, axis=-1, keepdims=True) + EPS)


def rms_back(x, gain, cot):
    r = inv_rms(x)
    t = cot * gain
    return r * (t - x * (r * r * jnp.mean(x * t, axis=-1, keepdims=True)))


def gelu_half(x):
    return 0.5 + 0.5 * jnp.tanh(x * (C0 + (C0 * C1) * (x * x)))


def gelu_slope(x):
    half = gelu_half(x)
    return half + (x * half) * (1.0 - half) * (2.0 * C0 + (6.0 * C0 * C1) * (x * x))


def head_masks(rows, heads_per_group, hdim):
    lane = lax.broadcasted_iota(jnp.int32, (rows, LANES), 1) // hdim
    return [(lane == h).astype(F32).astype(BF16) for h in range(heads_per_group)]


def arrange(even, from_a, from_b):
    return jnp.where(even, from_b, from_a), jnp.where(even, from_a, from_b)


def distances(ext, ext_t, first, d2_ref, count):
    for i in range(count):
        q = ext_t[(first + i) * BLK : (first + i + 1) * BLK]
        for s in range(3):
            k0 = (first + i - 1 + s) * BLK
            tot = None
            for c in range(3):
                diff = q[:, c : c + 1] - ext[c : c + 1, k0 : k0 + BLK]
                tot = diff * diff if tot is None else tot + diff * diff
            listed = ext[4 + s : 5 + s, (first + i) * BLK : (first + i + 1) * BLK] > 0.5
            d2_ref[i, :, s * BLK : (s + 1) * BLK] = jnp.where(listed, tot, FAR)


def stacked(x, masks):
    return jnp.concatenate([x * m for m in masks], axis=0)


def beside(x, y):
    zero = jnp.zeros_like(x)
    return jnp.concatenate([jnp.concatenate([x, zero], axis=1), jnp.concatenate([zero, y], axis=1)], axis=0)


def pair_products(a, b, masks2, per):
    each = [a * m for m in masks2]
    shared = mm_nt(jnp.concatenate(each, axis=0), b[BLK : 3 * BLK])
    both = jnp.concatenate([jnp.concatenate([x[:BLK], x[BLK:]], axis=1) for x in each], axis=0)
    outer = mm_nt(both, beside(b[:BLK], b[3 * BLK :]))
    got = []
    for t in range(2):
        got.append([
            (outer[h * BLK : (h + 1) * BLK, t * BLK : (t + 1) * BLK], shared[(2 * h + t) * BLK : (2 * h + t + 1) * BLK])
            for h in range(per)
        ])
    return got, each


def span(first, size, unit):
    if isinstance(first, int):
        return slice(first * unit, first * unit + size)
    return pl.ds(pl.multiple_of(first * unit, unit), size)


def blocks_at(first, count):
    return span(first, count * BLK, BLK)


def group_at(g):
    return span(g, LANES, LANES)


def over(pairs, groups, body, rolled=False):
    if rolled:
        lax.fori_loop(0, pairs * groups, lambda n, _: (body(2 * lax.div(n, groups), lax.rem(n, groups)), 0)[1], 0)
    else:
        for n in range(pairs * groups):
            body(2 * (n // groups), n % groups)


def window_parts(t):
    return (slice(0, BLK), slice(BLK, 3 * BLK)) if t == 0 else (slice(2 * BLK, 3 * BLK), slice(0, 2 * BLK))


def head_norms(x, hdim):
    width = x.shape[1]
    lane = lax.broadcasted_iota(jnp.int32, (width, LANES), 0) // hdim
    member = (lane == lax.broadcasted_iota(jnp.int32, (width, LANES), 1)).astype(F32).astype(BF16)
    x = x.astype(F32)
    return jnp.max(mm((x * x).astype(BF16), member), axis=0, keepdims=True)


def small_scores(q, k, hdim):
    return jnp.max(head_norms(q, hdim) * head_norms(k, hdim)) < 1600.0 * hdim


def attend(exact, q_ref, k_ref, vm_ref, o_ref, rl_ref, e_ref, d2_ref, d2_first, gam_ref, layer, heads, hdim, count):
    per = LANES // hdim
    groups = heads // per
    scale = hdim ** (-0.5)
    masks2 = head_masks(2 * BLK, per, hdim)
    ones2 = jnp.concatenate(masks2, axis=0)
    ones1 = jnp.concatenate([m[:BLK] for m in masks2], axis=0)

    def values(first, blocks, cols, ones):
        rows = blocks_at(first, blocks)
        return jnp.concatenate([jnp.concatenate([vm_ref[h, rows, cols] for h in range(per)], axis=0), ones], axis=1)

    def body(i, g):
        cols = group_at(g)
        scores, _ = pair_products(q_ref[blocks_at(i, 2), cols], k_ref[blocks_at(i, 4), cols], masks2, per)
        sides, middles = [], []
        for t in range(2):
            outer_cols, shared_cols = window_parts(t)
            outers, shareds = [], []
            for h in range(per):
                gam = gam_ref[layer, g * per + h, 0:1] / scale
                outer, shared = scores[t][h]
                outer = outer - gam * d2_ref[d2_first + i + t, :, outer_cols]
                shared = shared - jnp.concatenate([gam, gam], axis=1) * d2_ref[d2_first + i + t, :, shared_cols]
                if exact:
                    peak = jnp.maximum(jnp.maximum(outer, shared[:, :BLK]), shared[:, BLK:])
                    peak = jnp.max(peak, axis=1, keepdims=True)
                    outer, shared = outer - peak, shared - peak
                outer = jnp.exp(outer * scale).astype(BF16)
                shared = jnp.exp(shared * scale).astype(BF16)
                e_ref[i + t, g * per + h, :, outer_cols] = outer
                e_ref[i + t, g * per + h, :, shared_cols] = shared
                outers.append(outer)
                shareds.append(shared)
            middles.append(jnp.concatenate(shareds, axis=1))
            sides.append(mm(jnp.concatenate(outers, axis=1), values(i + 3 * t, 1, cols, ones1)))
        out = mm(jnp.concatenate(middles, axis=0), values(i + 1, 2, cols, ones2)) + jnp.concatenate(sides, axis=0)
        rl = 1.0 / jnp.maximum(out[:, LANES:], 1e-37)
        rl_ref[blocks_at(i, 2), cols] = rl
        o_ref[blocks_at(i, 2), cols] = (out[:, :LANES] * rl).astype(BF16)

    over(count // 2, groups, body, rolled=exact)


def split_heads(v_ref, vm_ref, hdim):
    rows, width = v_ref.shape
    masks = head_masks(BLK, LANES // hdim, hdim)
    for r in range(0, rows, BLK):
        for c in range(0, width, LANES):
            for h, m in enumerate(masks):
                vm_ref[h, r : r + BLK, c : c + LANES] = v_ref[r : r + BLK, c : c + LANES] * m


def delta_of(prod, per, hdim):
    lane = lax.broadcasted_iota(jnp.int32, prod.shape, 1) // hdim
    return [jnp.sum(jnp.where(lane == h, prod, 0.0), axis=1, keepdims=True) for h in range(per)]


def fold(grad, ext, ext_t, qb, kb):
    cols, rows = [], []
    for c in range(3):
        diff = ext_t[qb * BLK : (qb + 1) * BLK, c : c + 1] - ext[c : c + 1, kb * BLK : (kb + 1) * BLK]
        t = grad * diff
        cols.append(2.0 * jnp.sum(t, axis=1, keepdims=True))
        rows.append(-2.0 * jnp.sum(t, axis=0, keepdims=True))
    return cols, rows


def columns_to_rows(cols):
    lane = lax.broadcasted_iota(jnp.int32, (BLK, LANES), 1)
    wide = jnp.zeros((BLK, LANES), F32)
    for c in range(3):
        wide = jnp.where(lane == c, cols[c], wide)
    return wide.T[:8]


def three_rows(rows):
    sub = lax.broadcasted_iota(jnp.int32, (8, LANES), 0)
    out = jnp.zeros((8, LANES), F32)
    for c in range(3):
        out = jnp.where(sub == c, rows[c], out)
    return out


def pack_kernel(nb, me_ref, list_ref, pos_ref, spec_ref, own_ref, side_ref):
    own_ref[...] = jnp.zeros_like(own_ref)
    side_ref[...] = jnp.full(side_ref.shape, lax.rem(me_ref[0], 2).astype(F32))
    own_ref[0:3] = pos_ref[...]
    own_ref[3:4] = spec_ref[...].astype(F32)
    for b in range(nb):
        for s in range(3):
            listed = list_ref[b, s]
            ok = jnp.logical_and(listed == me_ref[0] * nb + (b - 1 + s), listed >= 0)
            own_ref[4 + s : 5 + s, b * BLK : (b + 1) * BLK] = jnp.full((1, BLK), ok.astype(F32))


def table_kernel(
    wq_h, embed_h, gains_h, wk_h, wv_h, gam_h, outg_h, ro_h,
    q_out, k_out, v_out, embed_out, gains_out, w_out, rates_out,
    wq, wk, wv, gam_ref, outg, ro, sem,
):
    pairs = (
        (embed_h, embed_out), (gains_h, gains_out), (wq_h.at[0], wq), (wk_h.at[0], wk), (wv_h.at[0], wv),
        (gam_h, gam_ref), (outg_h, outg), (ro_h, ro),
    )
    copies = [pltpu.make_async_copy(src, dst, sem.at[n]) for n, (src, dst) in enumerate(pairs)]
    for c in copies:
        c.start()
    for c in copies[:2]:
        c.wait()
    embed = embed_out[...].astype(F32)
    normed = (embed * inv_rms(embed) * gains_out[0, 0:1]).astype(BF16)
    for c in copies[2:]:
        c.wait()
    for w, out in ((wq, q_out), (wk, k_out), (wv, v_out)):
        out[...] = mm(normed, w[...]).astype(BF16)
    w_out[...] = jnp.broadcast_to(outg[...] * ro[...], w_out.shape)
    layers, heads = gam_ref.shape
    rates = gam_ref[...].T
    for layer in range(layers):
        for h in range(heads):
            rates_out[layer, h] = jnp.broadcast_to(rates[h : h + 1, layer : layer + 1], (8, LANES))


def first_kernel(
    nb, heads, hdim,
    par_ref, gam_ref, own_ref, ra_ref, rb_ref, qt_ref, kt_ref, vt_ref, embed_ref, gains_ref, w_ref,
    wq_h, wk_h, wv_h, wo_h, wu_h, wd_h,
    e_out, ext_ref, o_ref, rl_ref, v_ref, x1_ref, gd_ref, e_ref, wo0, wu0, wd0,
    st_ref, q1_ref, k1_ref, v1_ref, o1_ref, rl1_ref, e1_ref, x11_ref, gd1_ref, top_ref, wq1, wk1, wv1, wo1, wu1, wd1,
    d2_ref, x0_ref, q_ref, k_ref, vm_ref, vm1_ref, sem,
):
    qb = nb + 2
    kb = nb + 4
    mid = slice(BLK, (nb + 1) * BLK)
    sources = (wq_h, wk_h, wv_h, wo_h, wu_h, wd_h)
    targets = ((None, None, None, wo0, wu0, wd0), (wq1, wk1, wv1, wo1, wu1, wd1))
    copies = []
    for layer in range(2):
        copies.append([
            pltpu.make_async_copy(src.at[layer], dst, sem.at[layer, n])
            for n, (src, dst) in enumerate(zip(sources, targets[layer]))
            if dst is not None
        ])
        for c in copies[layer]:
            c.start()
    before, after = arrange(par_ref[0:1, 0:1] < 0.5, ra_ref[...], rb_ref[...])
    ext = jnp.concatenate([before, own_ref[...], after], axis=1)
    ext_ref[...] = ext
    ext_t = ext.T
    distances(ext, ext_t, 1, d2_ref, qb)

    scale = hdim ** (-0.5)
    spec = ext_t[:, 3:4].astype(jnp.int32)
    nspec = embed_ref.shape[0]
    onehot = (spec == lax.broadcasted_iota(jnp.int32, (kb * BLK, nspec), 1)).astype(F32).astype(BF16)
    onehot_q = onehot[BLK : (qb + 1) * BLK]
    x0_ref[...] = mm(onehot_q, embed_ref[...])
    q_ref[...] = mm(onehot_q, qt_ref[...]).astype(BF16)
    k_ref[...] = mm(onehot, kt_ref[...]).astype(BF16)
    v_ref[...] = mm(onehot, vt_ref[...]).astype(BF16)
    split_heads(v_ref, vm_ref, hdim)

    def run(exact):
        def arrived(some):
            if not exact:
                for c in some:
                    c.wait()

        attend(exact, q_ref, k_ref, vm_ref, o_ref, rl_ref, e_ref, d2_ref, 0, gam_ref, 0, heads, hdim, qb)

        arrived(copies[0])

        def feed(layer, x1, w_up, w_down, keep):
            inner = (x1 * inv_rms(x1) * gains_ref[layer, 1:2]).astype(BF16)
            pre = mm(inner, w_up[...])
            keep(pre)
            return x1 + mm((pre * gelu_half(pre)).astype(BF16), w_down[...])

        step = 4 * BLK
        for r in range(0, qb * BLK, step):
            rows = slice(r, r + step)
            x1 = x0_ref[rows] + mm(o_ref[rows], wo0[...])
            x1_ref[rows] = x1
            st_ref[rows] = feed(0, x1, wu0, wd0, lambda pre: gd_ref.__setitem__(rows, pre))

        arrived(copies[1])
        gain = gains_ref[1, 0:1]
        st = st_ref[...]
        normed = (st * inv_rms(st) * gain).astype(BF16)
        q1_ref[...] = mm(normed[mid], wq1[...]).astype(BF16)
        k1_ref[...] = mm(normed, wk1[...]).astype(BF16)
        v1_ref[...] = mm(normed, wv1[...]).astype(BF16)
        split_heads(v1_ref, vm1_ref, hdim)
        attend(exact, q1_ref, k1_ref, vm1_ref, o1_ref, rl1_ref, e1_ref, d2_ref, 1, gam_ref, 1, heads, hdim, nb)
        x1 = st_ref[mid] + mm(o1_ref[...], wo1[...])
        x11_ref[...] = x1
        x2 = feed(1, x1, wu1, wd1, lambda pre: gd1_ref.__setitem__(..., pre))

        w = w_ref[0:1]
        r = inv_rms(x2)
        along = jnp.sum(x2 * w, axis=1, keepdims=True)
        e_out[...] = jnp.broadcast_to(jnp.sum(along * r), e_out.shape)
        width = x2.shape[1]
        top_ref[...] = r * (w - x2 * (r * r * along * (1.0 / width)))

    run(False)
    small = jnp.logical_and(small_scores(qt_ref[...], kt_ref[...], hdim), small_scores(q1_ref[...], k1_ref[...], hdim))

    @pl.when(jnp.logical_not(small))
    def _():
        run(True)


def middle_kernel(
    nb, heads, hdim,
    par_ref, gam_ref, _, ext_ref, gains_ref, st_ref, q1_ref, k1_ref, v1_ref, o1_ref, rl1_ref, e1_ref, x1_ref, gd_ref, top_ref,
    wq, wk, wv, wo, wu, wd,
    paya_ref, payb_ref, part_ref, halo_ref, g1_ref,
    dq_ref, dk_ref, dv_ref, datt_ref,
):
    qb = nb + 2
    mid = slice(BLK, (nb + 1) * BLK)
    scale = hdim ** (-0.5)
    width = st_ref.shape[1]
    even = par_ref[0:1, 0:1] < 0.5
    ext = ext_ref[...]
    ext_t = ext.T
    grad = top_ref[...]
    du = mm_nt(grad.astype(BF16), wd[...]).astype(BF16).astype(F32)
    dinner = mm_nt((du * gelu_slope(gd_ref[...])).astype(BF16), wu[...]).astype(BF16).astype(F32)
    grad = grad + rms_back(x1_ref[...], gains_ref[1, 1:2], dinner)
    datt_ref[...] = mm_nt(grad.astype(BF16), wo[...]).astype(BF16).astype(F32)

    per = LANES // hdim
    groups = heads // per
    masks2 = head_masks(2 * BLK, per, hdim)
    masks3 = head_masks(3 * BLK, per, hdim)
    dk_ref[...] = jnp.zeros_like(dk_ref)
    dv_ref[...] = jnp.zeros_like(dv_ref)
    g1_ref[...] = jnp.zeros_like(g1_ref)

    def body(i, g):
        cols = group_at(g)
        rows2 = blocks_at(i, 2)
        d_o = datt_ref[rows2, cols] * rl1_ref[rows2, cols]
        delta = delta_of(d_o * o1_ref[rows2, cols].astype(F32), per, hdim)
        prods, each_do = pair_products(d_o.astype(BF16), v1_ref[blocks_at(i, 4), cols], masks2, per)
        q = q1_ref[rows2, cols]
        each_q = [q * m for m in masks2]
        es, dss = [], []
        for t in range(2):
            at = slice(t * BLK, (t + 1) * BLK)
            rows, win = blocks_at(i + t, 1), blocks_at(i + t, 3)
            outer_cols, shared_cols = window_parts(t)
            parts = []
            pair_outer = g1_ref[i + t, :, outer_cols]
            pair_shared = g1_ref[i + t, :, shared_cols]
            for h in range(per):
                e_outer, e_shared = e1_ref[i + t, g * per + h, :, outer_cols], e1_ref[i + t, g * per + h, :, shared_cols]
                outer, shared = prods[t][h]
                gam = gam_ref[1, g * per + h, 0:1]
                outer = e_outer.astype(F32) * (outer - delta[h][at])
                shared = e_shared.astype(F32) * (shared - delta[h][at])
                pair_outer = pair_outer + gam * outer
                pair_shared = pair_shared + jnp.concatenate([gam, gam], axis=1) * shared
                outer, shared = outer.astype(BF16), shared.astype(BF16)
                parts.append(jnp.concatenate([outer, shared] if t == 0 else [shared, outer], axis=1))
                es.append((e_outer, e_shared))
                dss.append((outer, shared))
            g1_ref[i + t, :, outer_cols] = pair_outer
            g1_ref[i + t, :, shared_cols] = pair_shared
            ks = stacked(k1_ref[win, cols], masks3)
            dq_ref[rows, cols] = (mm(jnp.concatenate(parts, axis=1), ks) * scale).astype(BF16)
        for ref, each, weights in ((dk_ref, each_q, dss), (dv_ref, each_do, es)):
            left = jnp.concatenate([x[t * BLK : (t + 1) * BLK] for t in range(2) for x in each], axis=0).T
            ref[cols, blocks_at(i + 1, 2)] += mm(left, jnp.concatenate([w[1] for w in weights], axis=0))
            for t in range(2):
                some = slice(t * per, (t + 1) * per)
                ref[cols, blocks_at(i + 3 * t, 1)] += mm(
                    left[:, t * per * BLK : (t + 1) * per * BLK], jnp.concatenate([w[0] for w in weights[some]], axis=0)
                )

    over(nb // 2, groups, body)
    dk = (dk_ref[...] * scale).astype(BF16).T
    dv = dv_ref[...].astype(BF16).T
    dnorm = mm_nt(dk, wk[...]) + mm_nt(dv, wv[...])
    dq = mm_nt(dq_ref[...], wq[...])
    zeros = jnp.zeros((BLK, width), F32)
    dnorm = dnorm + jnp.concatenate([zeros, dq, zeros], axis=0)
    back = rms_back(st_ref[...], gains_ref[1, 0:1], dnorm.astype(BF16).astype(F32))
    part = grad + back[mid]
    part_ref[...] = part
    halo_ref[:BLK] = back[:BLK]
    halo_ref[BLK:] = back[(qb - 1) * BLK :]

    _, rows_low = fold(g1_ref[0, :, :BLK], ext, ext_t, 2, 1)
    _, rows_high = fold(g1_ref[nb - 1, :, 2 * BLK :], ext, ext_t, nb + 1, nb + 2)
    pad = jnp.zeros((8, width - LANES), F32)

    def payload(halo, edge, rows):
        tail = jnp.concatenate([three_rows(rows), pad], axis=1)
        return halo, edge, jnp.concatenate([tail, jnp.zeros_like(tail)], axis=0)

    low = payload(back[:BLK], part[:BLK], rows_low)
    high = payload(back[(qb - 1) * BLK :], part[(nb - 1) * BLK :], rows_high)
    at = 0
    for x, y in zip(high, low):
        rows = slice(at, at + x.shape[0])
        paya_ref[rows] = jnp.where(even, x, y).astype(BF16)
        payb_ref[rows] = jnp.where(even, y, x).astype(BF16)
        at += x.shape[0]


def slope_kernel(_, pre_ref, out_ref):
    out_ref[...] = gelu_slope(pre_ref[...]).astype(BF16)


def last_kernel(
    nb, heads, hdim,
    par_ref, gam_ref, energy_ref, ext_ref, gains_ref, paya_ref, payb_ref, part_ref, halo_ref, g1_ref,
    o_ref, rl_ref, v_ref, x1_ref, gd_ref, e_ref, wo, wu, wd,
    f_ref,
    datt_ref, sum_ref, ends_ref,
):
    qb = nb + 2
    ext = ext_ref[...]
    ext_t = ext.T

    even = par_ref[0:1, 0:1] < 0.5
    from_a, from_b = paya_ref[...].astype(F32), payb_ref[...].astype(F32)
    from_low, from_high = arrange(even, from_a, from_b)
    part = part_ref[...]
    pieces = [halo_ref[:BLK] + from_low[BLK : 2 * BLK]]
    own_parts = [part[i * BLK : (i + 1) * BLK] for i in range(nb)]
    own_parts[0] = own_parts[0] + from_low[:BLK]
    own_parts[-1] = own_parts[-1] + from_high[:BLK]
    pieces += own_parts
    pieces.append(halo_ref[BLK:] + from_high[BLK : 2 * BLK])
    grad = jnp.concatenate(pieces, axis=0)
    du = mm_nt(grad.astype(BF16), wd[...]).astype(BF16).astype(F32)
    dinner = mm_nt((du * gd_ref[...].astype(F32)).astype(BF16), wu[...]).astype(BF16).astype(F32)
    grad = grad + rms_back(x1_ref[...], gains_ref[0, 1:2], dinner)
    datt_ref[...] = mm_nt(grad.astype(BF16), wo[...]).astype(BF16).astype(F32)

    per = LANES // hdim
    groups = heads // per
    masks = head_masks(BLK, per, hdim)
    masks2 = head_masks(2 * BLK, per, hdim)

    def cotangents(rows, g):
        cols = group_at(g)
        lane = lax.broadcasted_iota(jnp.int32, (1, LANES), 1) // hdim
        gam = jnp.zeros((1, LANES), F32)
        for h in range(per):
            gam = jnp.where(lane == h, gam_ref[0, g * per + h, 0:1], gam)
        d_o = datt_ref[rows, cols] * rl_ref[rows, cols] * gam
        return d_o.astype(BF16), delta_of(d_o * o_ref[rows, cols].astype(F32), per, hdim)

    last = qb - 1
    sum_ref[...] = g1_ref[...]
    ends_ref[...] = jnp.zeros_like(ends_ref)

    def body(i, g):
        d_o, delta = cotangents(blocks_at(i + 1, 2), g)
        prods, _ = pair_products(d_o, v_ref[blocks_at(i + 1, 4), group_at(g)], masks2, per)
        for t in range(2):
            at = slice(t * BLK, (t + 1) * BLK)
            for n, c in enumerate(window_parts(t)):
                total = sum_ref[i + t, :, c]
                for h in range(per):
                    total = total + e_ref[i + t + 1, g * per + h, :, c].astype(F32) * (prods[t][h][n] - delta[h][at])
                sum_ref[i + t, :, c] = total

    def ends(_, g):
        cols = group_at(g)
        low_o, low_delta = cotangents(slice(0, BLK), g)
        high_o, high_delta = cotangents(slice(last * BLK, qb * BLK), g)
        both = jnp.concatenate([low_o, high_o], axis=1)
        both = jnp.concatenate([both * jnp.concatenate([m, m], axis=1) for m in masks], axis=0)
        prods = mm_nt(both, beside(v_ref[2 * BLK : 3 * BLK, cols], v_ref[last * BLK : qb * BLK, cols]))
        low_sum, high_sum = ends_ref[0], ends_ref[1]
        for h in range(per):
            low = prods[h * BLK : (h + 1) * BLK, :BLK] - low_delta[h]
            high = prods[h * BLK : (h + 1) * BLK, BLK:] - high_delta[h]
            low_sum = low_sum + e_ref[0, g * per + h, :, 2 * BLK :].astype(F32) * low
            high_sum = high_sum + e_ref[last, g * per + h, :, :BLK].astype(F32) * high
        ends_ref[0] = low_sum
        ends_ref[1] = high_sum

    over(nb // 2, groups, body)
    over(1, groups, ends)
    forces = [jnp.zeros((8, LANES), F32) for _ in range(nb)]
    forces[0] = forces[0] + from_low[2 * BLK : 2 * BLK + 8, :LANES]
    forces[-1] = forces[-1] + from_high[2 * BLK : 2 * BLK + 8, :LANES]
    for i in range(nb):
        total = sum_ref[i]
        sums = None
        for s in range(3):
            cols, rows = fold(total[:, s * BLK : (s + 1) * BLK], ext, ext_t, i + 2, i + 1 + s)
            sums = cols if sums is None else [a + b for a, b in zip(sums, cols)]
            j = i - 1 + s
            if 0 <= j < nb:
                forces[j] = forces[j] + three_rows(rows)
        forces[i] = forces[i] + columns_to_rows(sums)
    _, rows = fold(ends_ref[0], ext, ext_t, 1, 2)
    forces[0] = forces[0] + three_rows(rows)
    _, rows = fold(ends_ref[1], ext, ext_t, nb + 2, nb + 1)
    forces[-1] = forces[-1] + three_rows(rows)
    f_ref[...] = jnp.concatenate(forces, axis=1)[:3]


def swap_a(x):
    n = lax.axis_size("chain")
    return lax.ppermute(x, "chain", [(i, i ^ 1) for i in range(n)])


def swap_b(x):
    n = lax.axis_size("chain")
    return lax.ppermute(x, "chain", [(i, ((i + 1) ^ 1) - 1) for i in range(1, n - 1)])


def hop(x, step):
    return lax.ppermute(x, "chain", [(i, i ^ step) for i in range(lax.axis_size("chain"))])


def local(
    species, positions, block_list, embed, w_query, w_key, w_value, w_out, w_up, w_down, norm_gains, gammas, out_gain, readout
):
    atoms = species.shape[0]
    nb = atoms // BLK
    width = embed.shape[1]
    layers, heads = gammas.shape
    hdim = width // heads
    ff = w_up.shape[2]
    qb, kb = nb + 2, nb + 4
    count = lax.axis_size("chain")
    assert nb >= 2 and layers == 2 and LANES % hdim == 0 and nb % 2 == 0 and count >= 8 and count & (count - 1) == 0
    me = lax.axis_index("chain").astype(jnp.int32)
    vm = pltpu.VMEM
    smem = pl.BlockSpec(memory_space=pltpu.SMEM)

    def work(products):
        return pl.CostEstimate(flops=products * atoms * width * width * 8, transcendentals=0, bytes_accessed=0)

    vmem = pl.BlockSpec(memory_space=vm)
    keep = functools.partial(pltpu.with_memory_space_constraint, memory_space=vm)
    pin = functools.partial(pltpu.with_memory_space_constraint, memory_space=pltpu.HBM)
    own, side = pl.pallas_call(
        functools.partial(pack_kernel, nb),
        out_shape=[vm((8, atoms), F32), vm((8, LANES), F32)],
        in_specs=[smem, smem, vmem, vmem],
        out_specs=[vmem, vmem],
    )(me.reshape(1), block_list, positions, species.reshape(1, atoms))
    edge = 2 * BLK
    if atoms == edge:
        send_a = send_b = own
    else:
        first, last = own[:, :edge], own[:, -edge:]
        send_a = jnp.where(me % 2 == 0, last, first)
        send_b = jnp.where(me % 2 == 0, first, last)
    near_a, near_b = swap_a(send_a), swap_b(send_b)
    hbm = pl.BlockSpec(memory_space=pltpu.HBM)
    table = vm(embed.shape, BF16)
    square = vm((width, width), BF16)
    small = pl.pallas_call(
        table_kernel,
        out_shape=[
            table, table, table, table, vm(norm_gains.shape, F32), vm((8, width), F32),
            vm((layers, heads, 8, LANES), F32),
        ],
        in_specs=[hbm] * 8,
        out_specs=[vmem] * 7,
        scratch_shapes=[
            square, square, square, vm((layers, heads), F32), vm((1, width), F32), vm((1, width), F32),
            pltpu.SemaphoreType.DMA((8,)),
        ],
        compiler_params=pltpu.CompilerParams(vmem_limit_bytes=8 * 1024 * 1024),
        cost_estimate=work(1),
    )(
        pin(w_query), pin(embed), pin(norm_gains), pin(w_key), pin(w_value), pin(gammas),
        pin(out_gain.reshape(1, width)), pin(readout.reshape(1, width)),
    )
    *tables, gains, w, rates = (keep(x) for x in small)
    side = keep(side)
    weights = (w_query, w_key, w_value, w_out, w_up, w_down)
    shapes = [vm((width, width), BF16)] * 4 + [vm((width, ff), BF16), vm((ff, width), BF16)]
    first = pl.pallas_call(
        functools.partial(first_kernel, nb, heads, hdim),
        out_shape=[
            vm((8, LANES), F32), vm((8, kb * BLK), F32),
            vm((qb * BLK, width), BF16), vm((qb * BLK, width), F32), vm((kb * BLK, width), BF16),
            vm((qb * BLK, width), F32), vm((qb * BLK, ff), F32), vm((qb, heads, BLK, 3 * BLK), BF16), *shapes[3:],
            vm((qb * BLK, width), F32), vm((nb * BLK, width), BF16), vm((qb * BLK, width), BF16),
            vm((qb * BLK, width), BF16), vm((nb * BLK, width), BF16), vm((nb * BLK, width), F32),
            vm((nb, heads, BLK, 3 * BLK), BF16), vm((nb * BLK, width), F32), vm((nb * BLK, ff), F32),
            vm((nb * BLK, width), F32), *shapes,
        ],
        in_specs=[vmem] * 11 + [hbm] * 6,
        out_specs=[vmem] * 27,
        scratch_shapes=[
            vm((qb, BLK, 3 * BLK), F32), vm((qb * BLK, width), F32), vm((qb * BLK, width), BF16),
            vm((kb * BLK, width), BF16), vm((LANES // hdim, kb * BLK, width), BF16),
            vm((LANES // hdim, qb * BLK, width), BF16), pltpu.SemaphoreType.DMA((2, 6)),
        ],
        compiler_params=pltpu.CompilerParams(vmem_limit_bytes=20 * 1024 * 1024),
        cost_estimate=work(qb * 7),
    )(
        side, rates, keep(own), keep(near_a), keep(near_b), *tables, gains, w, *(pin(x) for x in weights),
    )
    energy, ext = first[0], keep(first[1])
    saved0 = [keep(x) for x in first[2:11]]
    saved1 = [keep(x) for x in first[11:]]
    energy = energy + hop(energy, 1)
    pay = vm((2 * BLK + 16, width), BF16)
    pay_a, pay_b, part, halo, pairs = pl.pallas_call(
        functools.partial(middle_kernel, nb, heads, hdim),
        out_shape=[pay, pay, vm((nb * BLK, width), F32), vm((2 * BLK, width), F32), vm((nb, BLK, 3 * BLK), F32)],
        in_specs=[vmem] * 21,
        out_specs=[vmem] * 5,
        scratch_shapes=[
            vm((nb * BLK, width), BF16), vm((width, qb * BLK), F32), vm((width, qb * BLK), F32), vm((nb * BLK, width), F32),
        ],
        compiler_params=pltpu.CompilerParams(vmem_limit_bytes=20 * 1024 * 1024),
        cost_estimate=work(nb * 9),
    )(side, rates, keep(energy), ext, gains, *saved1)
    energy = energy + hop(energy, 2)
    energy, pay_a, pay_b = lax.optimization_barrier((energy, pay_a, pay_b))
    saved0[4] = keep(
        pl.pallas_call(
            slope_kernel,
            out_shape=vm((qb * BLK, ff), BF16),
            in_specs=[vmem, vmem],
            out_specs=vmem,
            compiler_params=pltpu.CompilerParams(vmem_limit_bytes=8 * 1024 * 1024),
            cost_estimate=work(qb),
        )(keep(energy), saved0[4])
    )
    arriving = hop(energy, 4)
    got_a, got_b = swap_a(pay_a), swap_b(pay_b)
    energy = energy + arriving
    forces = pl.pallas_call(
        functools.partial(last_kernel, nb, heads, hdim),
        out_shape=jax.ShapeDtypeStruct((3, atoms), F32),
        in_specs=[vmem] * 19,
        out_specs=vmem,
        scratch_shapes=[vm((qb * BLK, width), F32), vm((nb, BLK, 3 * BLK), F32), vm((2, BLK, BLK), F32)],
        compiler_params=pltpu.CompilerParams(vmem_limit_bytes=20 * 1024 * 1024),
        cost_estimate=work(qb * 3),
    )(
        side, rates, keep(energy), ext, gains, keep(got_a), keep(got_b), keep(part), keep(halo), keep(pairs), *saved0
    )
    if count > 8:
        arriving = hop(energy, 8)
        energy, forces = lax.optimization_barrier((energy, forces))
        energy = energy + arriving
    step = 16
    while step < count:
        energy = energy + hop(energy, step)
        step *= 2
    return energy[:1, :1].reshape(1), forces


def solution(mesh):
    sharded = ("frames", "chain")
    return jax.shard_map(
        local,
        mesh=mesh,
        in_specs=(P(sharded), P(None, sharded), P(sharded, None)) + (P(),) * 11,
        out_specs=(P("frames"), P(None, sharded)),
        check_vma=False,
    )
```

```python
import functools
import math

import jax
import jax.numpy as jnp
from jax import lax
from jax.experimental import pallas as pl
from jax.experimental.pallas import tpu as pltpu
from jax.sharding import PartitionSpec as P

BLK = 128
LANES = 128
EPS = 1e-06
FAR = 1e30
F32 = jnp.float32
BF16 = jnp.bfloat16
C0 = math.sqrt(2.0 / math.pi)
C1 = 0.044715


def mm(a, b):
    return jnp.dot(a, b, preferred_element_type=F32)


def mm_nt(a, b):
    return lax.dot_general(a, b, (((1,), (1,)), ((), ())), preferred_element_type=F32)


def mm_tn(a, b):
    return lax.dot_general(a, b, (((0,), (0,)), ((), ())), preferred_element_type=F32)


def inv_rms(x):
    return lax.rsqrt(jnp.mean(x * x, axis=-1, keepdims=True) + EPS)


def rms_back(x, gain, cot):
    r = inv_rms(x)
    t = cot * gain
    return r * (t - x * (r * r * jnp.mean(x * t, axis=-1, keepdims=True)))


def gelu_half(x):
    return 0.5 + 0.5 * jnp.tanh(x * (C0 + (C0 * C1) * (x * x)))


def gelu_slope(x):
    half = gelu_half(x)
    return half + (x * half) * (1.0 - half) * (2.0 * C0 + (6.0 * C0 * C1) * (x * x))


def head_masks(rows, heads_per_group, hdim):
    lane = lax.broadcasted_iota(jnp.int32, (rows, LANES), 1) // hdim
    return [(lane == h).astype(F32).astype(BF16) for h in range(heads_per_group)]


def arrange(even, from_a, from_b):
    return jnp.where(even, from_b, from_a), jnp.where(even, from_a, from_b)


def distances(ext, ext_t, first, d2_ref, count):
    for i in range(count):
        q = ext_t[(first + i) * BLK : (first + i + 1) * BLK]
        for s in range(3):
            k0 = (first + i - 1 + s) * BLK
            tot = None
            for c in range(3):
                diff = q[:, c : c + 1] - ext[c : c + 1, k0 : k0 + BLK]
                tot = diff * diff if tot is None else tot + diff * diff
            listed = ext[4 + s : 5 + s, (first + i) * BLK : (first + i + 1) * BLK] > 0.5
            d2_ref[i, :, s * BLK : (s + 1) * BLK] = jnp.where(listed, tot, FAR)


def stacked(x, masks):
    return jnp.concatenate([x * m for m in masks], axis=0)


def beside(x, y):
    zero = jnp.zeros_like(x)
    return jnp.concatenate([jnp.concatenate([x, zero], axis=1), jnp.concatenate([zero, y], axis=1)], axis=0)


def pair_products(a, b, masks2, per):
    each = [a * m for m in masks2]
    shared = mm_nt(jnp.concatenate(each, axis=0), b[BLK : 3 * BLK])
    both = jnp.concatenate([jnp.concatenate([x[:BLK], x[BLK:]], axis=1) for x in each], axis=0)
    outer = mm_nt(both, beside(b[:BLK], b[3 * BLK :]))
    got = []
    for t in range(2):
        got.append([
            (outer[h * BLK : (h + 1) * BLK, t * BLK : (t + 1) * BLK], shared[(2 * h + t) * BLK : (2 * h + t + 1) * BLK])
            for h in range(per)
        ])
    return got, each


def span(first, size, unit):
    if isinstance(first, int):
        return slice(first * unit, first * unit + size)
    return pl.ds(pl.multiple_of(first * unit, unit), size)


def blocks_at(first, count):
    return span(first, count * BLK, BLK)


def group_at(g):
    return span(g, LANES, LANES)


def over(pairs, groups, body, rolled=False):
    if rolled:
        lax.fori_loop(0, pairs * groups, lambda n, _: (body(2 * lax.div(n, groups), lax.rem(n, groups)), 0)[1], 0)
    else:
        for n in range(pairs * groups):
            body(2 * (n // groups), n % groups)


def window_parts(t):
    return (slice(0, BLK), slice(BLK, 3 * BLK)) if t == 0 else (slice(2 * BLK, 3 * BLK), slice(0, 2 * BLK))


def head_norms(x, hdim):
    width = x.shape[1]
    lane = lax.broadcasted_iota(jnp.int32, (width, LANES), 0) // hdim
    member = (lane == lax.broadcasted_iota(jnp.int32, (width, LANES), 1)).astype(F32).astype(BF16)
    x = x.astype(F32)
    return jnp.max(mm((x * x).astype(BF16), member), axis=0, keepdims=True)


def small_scores(q, k, hdim):
    return jnp.max(head_norms(q, hdim) * head_norms(k, hdim)) < 1600.0 * hdim


def attend(exact, q_ref, k_ref, vm_ref, o_ref, rl_ref, e_ref, d2_ref, d2_first, gam_ref, layer, heads, hdim, count):
    per = LANES // hdim
    groups = heads // per
    scale = hdim ** (-0.5)
    masks2 = head_masks(2 * BLK, per, hdim)
    ones2 = jnp.concatenate(masks2, axis=0)
    ones1 = jnp.concatenate([m[:BLK] for m in masks2], axis=0)

    def values(first, blocks, cols, ones):
        rows = blocks_at(first, blocks)
        return jnp.concatenate([jnp.concatenate([vm_ref[h, rows, cols] for h in range(per)], axis=0), ones], axis=1)

    def body(i, g):
        cols = group_at(g)
        scores, _ = pair_products(q_ref[blocks_at(i, 2), cols], k_ref[blocks_at(i, 4), cols], masks2, per)
        sides, middles = [], []
        for t in range(2):
            outer_cols, shared_cols = window_parts(t)
            outers, shareds = [], []
            for h in range(per):
                gam = gam_ref[layer, g * per + h, 0:1] / scale
                outer, shared = scores[t][h]
                outer = outer - gam * d2_ref[d2_first + i + t, :, outer_cols]
                shared = shared - jnp.concatenate([gam, gam], axis=1) * d2_ref[d2_first + i + t, :, shared_cols]
                if exact:
                    peak = jnp.maximum(jnp.maximum(outer, shared[:, :BLK]), shared[:, BLK:])
                    peak = jnp.max(peak, axis=1, keepdims=True)
                    outer, shared = outer - peak, shared - peak
                outer = jnp.exp(outer * scale).astype(BF16)
                shared = jnp.exp(shared * scale).astype(BF16)
                e_ref[i + t, g * per + h, :, outer_cols] = outer
                e_ref[i + t, g * per + h, :, shared_cols] = shared
                outers.append(outer)
                shareds.append(shared)
            middles.append(jnp.concatenate(shareds, axis=1))
            sides.append(mm(jnp.concatenate(outers, axis=1), values(i + 3 * t, 1, cols, ones1)))
        out = mm(jnp.concatenate(middles, axis=0), values(i + 1, 2, cols, ones2)) + jnp.concatenate(sides, axis=0)
        rl = 1.0 / jnp.maximum(out[:, LANES:], 1e-37)
        rl_ref[blocks_at(i, 2), cols] = rl
        o_ref[blocks_at(i, 2), cols] = (out[:, :LANES] * rl).astype(BF16)

    over(count // 2, groups, body, rolled=exact)


def split_heads(v_ref, vm_ref, hdim):
    rows, width = v_ref.shape
    masks = head_masks(BLK, LANES // hdim, hdim)
    for r in range(0, rows, BLK):
        for c in range(0, width, LANES):
            for h, m in enumerate(masks):
                vm_ref[h, r : r + BLK, c : c + LANES] = v_ref[r : r + BLK, c : c + LANES] * m


def delta_of(prod, per, hdim):
    lane = lax.broadcasted_iota(jnp.int32, prod.shape, 1) // hdim
    return [jnp.sum(jnp.where(lane == h, prod, 0.0), axis=1, keepdims=True) for h in range(per)]


def fold(grad, ext, ext_t, qb, kb):
    cols, rows = [], []
    for c in range(3):
        diff = ext_t[qb * BLK : (qb + 1) * BLK, c : c + 1] - ext[c : c + 1, kb * BLK : (kb + 1) * BLK]
        t = grad * diff
        cols.append(2.0 * jnp.sum(t, axis=1, keepdims=True))
        rows.append(-2.0 * jnp.sum(t, axis=0, keepdims=True))
    return cols, rows


def columns_to_rows(cols):
    lane = lax.broadcasted_iota(jnp.int32, (BLK, LANES), 1)
    wide = jnp.zeros((BLK, LANES), F32)
    for c in range(3):
        wide = jnp.where(lane == c, cols[c], wide)
    return wide.T[:8]


def three_rows(rows):
    sub = lax.broadcasted_iota(jnp.int32, (8, LANES), 0)
    out = jnp.zeros((8, LANES), F32)
    for c in range(3):
        out = jnp.where(sub == c, rows[c], out)
    return out


def pack_kernel(nb, me_ref, list_ref, pos_ref, spec_ref, own_ref, side_ref):
    own_ref[...] = jnp.zeros_like(own_ref)
    side_ref[...] = jnp.full(side_ref.shape, lax.rem(me_ref[0], 2).astype(F32))
    own_ref[0:3] = pos_ref[...]
    own_ref[3:4] = spec_ref[...].astype(F32)
    for b in range(nb):
        for s in range(3):
            listed = list_ref[b, s]
            ok = jnp.logical_and(listed == me_ref[0] * nb + (b - 1 + s), listed >= 0)
            own_ref[4 + s : 5 + s, b * BLK : (b + 1) * BLK] = jnp.full((1, BLK), ok.astype(F32))


def table_kernel(
    wq_h, embed_h, gains_h, wk_h, wv_h, gam_h, outg_h, ro_h,
    q_out, k_out, v_out, embed_out, gains_out, w_out, rates_out,
    wq, wk, wv, gam_ref, outg, ro, sem,
):
    pairs = (
        (embed_h, embed_out), (gains_h, gains_out), (wq_h.at[0], wq), (wk_h.at[0], wk), (wv_h.at[0], wv),
        (gam_h, gam_ref), (outg_h, outg), (ro_h, ro),
    )
    copies = [pltpu.make_async_copy(src, dst, sem.at[n]) for n, (src, dst) in enumerate(pairs)]
    for c in copies:
        c.start()
    for c in copies[:2]:
        c.wait()
    embed = embed_out[...].astype(F32)
    normed = (embed * inv_rms(embed) * gains_out[0, 0:1]).astype(BF16)
    for c in copies[2:]:
        c.wait()
    for w, out in ((wq, q_out), (wk, k_out), (wv, v_out)):
        out[...] = mm(normed, w[...]).astype(BF16)
    w_out[...] = jnp.broadcast_to(outg[...] * ro[...], w_out.shape)
    layers, heads = gam_ref.shape
    rates = gam_ref[...].T
    for layer in range(layers):
        for h in range(heads):
            rates_out[layer, h] = jnp.broadcast_to(rates[h : h + 1, layer : layer + 1], (8, LANES))


def first_kernel(
    nb, heads, hdim,
    par_ref, gam_ref, own_ref, ra_ref, rb_ref, qt_ref, kt_ref, vt_ref, embed_ref, gains_ref, w_ref,
    wq_h, wk_h, wv_h, wo_h, wu_h, wd_h,
    e_out, ext_ref, o_ref, rl_ref, v_ref, x1_ref, gd_ref, e_ref, wo0, wu0, wd0,
    st_ref, q1_ref, k1_ref, v1_ref, o1_ref, rl1_ref, e1_ref, x11_ref, gd1_ref, top_ref, wq1, wk1, wv1, wo1, wu1, wd1,
    d2_ref, x0_ref, q_ref, k_ref, vm_ref, vm1_ref, sem,
):
    qb = nb + 2
    kb = nb + 4
    mid = slice(BLK, (nb + 1) * BLK)
    sources = (wq_h, wk_h, wv_h, wo_h, wu_h, wd_h)
    targets = ((None, None, None, wo0, wu0, wd0), (wq1, wk1, wv1, wo1, wu1, wd1))
    copies = []
    for layer in range(2):
        copies.append([
            pltpu.make_async_copy(src.at[layer], dst, sem.at[layer, n])
            for n, (src, dst) in enumerate(zip(sources, targets[layer]))
            if dst is not None
        ])
        for c in copies[layer]:
            c.start()
    before, after = arrange(par_ref[0:1, 0:1] < 0.5, ra_ref[...], rb_ref[...])
    ext = jnp.concatenate([before, own_ref[...], after], axis=1)
    ext_ref[...] = ext
    ext_t = ext.T
    distances(ext, ext_t, 1, d2_ref, qb)

    scale = hdim ** (-0.5)
    spec = ext_t[:, 3:4].astype(jnp.int32)
    nspec = embed_ref.shape[0]
    onehot = (spec == lax.broadcasted_iota(jnp.int32, (kb * BLK, nspec), 1)).astype(F32).astype(BF16)
    onehot_q = onehot[BLK : (qb + 1) * BLK]
    x0_ref[...] = mm(onehot_q, embed_ref[...])
    q_ref[...] = mm(onehot_q, qt_ref[...]).astype(BF16)
    k_ref[...] = mm(onehot, kt_ref[...]).astype(BF16)
    v_ref[...] = mm(onehot, vt_ref[...]).astype(BF16)
    split_heads(v_ref, vm_ref, hdim)

    def run(exact):
        def arrived(some):
            if not exact:
                for c in some:
                    c.wait()

        attend(exact, q_ref, k_ref, vm_ref, o_ref, rl_ref, e_ref, d2_ref, 0, gam_ref, 0, heads, hdim, qb)

        arrived(copies[0])

        def feed(layer, x1, w_up, w_down, keep):
            inner = (x1 * inv_rms(x1) * gains_ref[layer, 1:2]).astype(BF16)
            pre = mm(inner, w_up[...])
            keep(pre)
            return x1 + mm((pre * gelu_half(pre)).astype(BF16), w_down[...])

        step = 4 * BLK
        for r in range(0, qb * BLK, step):
            rows = slice(r, r + step)
            x1 = x0_ref[rows] + mm(o_ref[rows], wo0[...])
            x1_ref[rows] = x1
            st_ref[rows] = feed(0, x1, wu0, wd0, lambda pre: gd_ref.__setitem__(rows, pre))

        arrived(copies[1])
        gain = gains_ref[1, 0:1]
        st = st_ref[...]
        normed = (st * inv_rms(st) * gain).astype(BF16)
        q1_ref[...] = mm(normed[mid], wq1[...]).astype(BF16)
        k1_ref[...] = mm(normed, wk1[...]).astype(BF16)
        v1_ref[...] = mm(normed, wv1[...]).astype(BF16)
        split_heads(v1_ref, vm1_ref, hdim)
        attend(exact, q1_ref, k1_ref, vm1_ref, o1_ref, rl1_ref, e1_ref, d2_ref, 1, gam_ref, 1, heads, hdim, nb)
        x1 = st_ref[mid] + mm(o1_ref[...], wo1[...])
        x11_ref[...] = x1
        x2 = feed(1, x1, wu1, wd1, lambda pre: gd1_ref.__setitem__(..., pre))

        w = w_ref[0:1]
        r = inv_rms(x2)
        along = jnp.sum(x2 * w, axis=1, keepdims=True)
        e_out[...] = jnp.broadcast_to(jnp.sum(along * r), e_out.shape)
        width = x2.shape[1]
        top_ref[...] = r * (w - x2 * (r * r * along * (1.0 / width)))

    run(False)
    small = jnp.logical_and(small_scores(qt_ref[...], kt_ref[...], hdim), small_scores(q1_ref[...], k1_ref[...], hdim))

    @pl.when(jnp.logical_not(small))
    def _():
        run(True)


def feed_back_kernel(gains_ref, x1_ref, gd_ref, top_ref, wo, wu, wd, grad_ref, datt_ref):
    grad = top_ref[...]
    du = mm_nt(grad.astype(BF16), wd[...]).astype(BF16).astype(F32)
    dinner = mm_nt((du * gelu_slope(gd_ref[...])).astype(BF16), wu[...]).astype(BF16).astype(F32)
    grad = grad + rms_back(x1_ref[...], gains_ref[1, 1:2], dinner)
    grad_ref[...] = grad
    datt_ref[...] = mm_nt(grad.astype(BF16), wo[...]).astype(BF16).astype(F32)


def middle_kernel(
    nb, heads, hdim,
    par_ref, gam_ref, _, ext_ref, gains_ref, st_ref, q1_ref, k1_ref, v1_ref, o1_ref, rl1_ref, e1_ref, grad_ref, datt_ref,
    wq, wk, wv,
    paya_ref, payb_ref, part_ref, halo_ref, g1_ref,
    dq_ref, dk_ref, dv_ref,
):
    qb = nb + 2
    mid = slice(BLK, (nb + 1) * BLK)
    scale = hdim ** (-0.5)
    width = st_ref.shape[1]
    even = par_ref[0:1, 0:1] < 0.5
    ext = ext_ref[...]
    ext_t = ext.T
    grad = grad_ref[...]

    per = LANES // hdim
    groups = heads // per
    masks2 = head_masks(2 * BLK, per, hdim)
    masks3 = head_masks(3 * BLK, per, hdim)
    dk_ref[...] = jnp.zeros_like(dk_ref)
    dv_ref[...] = jnp.zeros_like(dv_ref)
    g1_ref[...] = jnp.zeros_like(g1_ref)

    def body(i, g):
        cols = group_at(g)
        rows2 = blocks_at(i, 2)
        d_o = datt_ref[rows2, cols] * rl1_ref[rows2, cols]
        delta = delta_of(d_o * o1_ref[rows2, cols].astype(F32), per, hdim)
        prods, each_do = pair_products(d_o.astype(BF16), v1_ref[blocks_at(i, 4), cols], masks2, per)
        q = q1_ref[rows2, cols]
        each_q = [q * m for m in masks2]
        es, dss = [], []
        for t in range(2):
            at = slice(t * BLK, (t + 1) * BLK)
            rows, win = blocks_at(i + t, 1), blocks_at(i + t, 3)
            outer_cols, shared_cols = window_parts(t)
            parts = []
            pair_outer = g1_ref[i + t, :, outer_cols]
            pair_shared = g1_ref[i + t, :, shared_cols]
            for h in range(per):
                e_outer, e_shared = e1_ref[i + t, g * per + h, :, outer_cols], e1_ref[i + t, g * per + h, :, shared_cols]
                outer, shared = prods[t][h]
                gam = gam_ref[1, g * per + h, 0:1]
                outer = e_outer.astype(F32) * (outer - delta[h][at])
                shared = e_shared.astype(F32) * (shared - delta[h][at])
                pair_outer = pair_outer + gam * outer
                pair_shared = pair_shared + jnp.concatenate([gam, gam], axis=1) * shared
                outer, shared = outer.astype(BF16), shared.astype(BF16)
                parts.append(jnp.concatenate([outer, shared] if t == 0 else [shared, outer], axis=1))
                es.append((e_outer, e_shared))
                dss.append((outer, shared))
            g1_ref[i + t, :, outer_cols] = pair_outer
            g1_ref[i + t, :, shared_cols] = pair_shared
            ks = stacked(k1_ref[win, cols], masks3)
            dq_ref[rows, cols] = (mm(jnp.concatenate(parts, axis=1), ks) * scale).astype(BF16)
        for ref, each, weights in ((dk_ref, each_q, dss), (dv_ref, each_do, es)):
            left = jnp.concatenate([x[t * BLK : (t + 1) * BLK] for t in range(2) for x in each], axis=0).T
            ref[cols, blocks_at(i + 1, 2)] += mm(left, jnp.concatenate([w[1] for w in weights], axis=0))
            for t in range(2):
                some = slice(t * per, (t + 1) * per)
                ref[cols, blocks_at(i + 3 * t, 1)] += mm(
                    left[:, t * per * BLK : (t + 1) * per * BLK], jnp.concatenate([w[0] for w in weights[some]], axis=0)
                )

    over(nb // 2, groups, body)
    dk = (dk_ref[...] * scale).astype(BF16).T
    dv = dv_ref[...].astype(BF16).T
    dnorm = mm_nt(dk, wk[...]) + mm_nt(dv, wv[...])
    dq = mm_nt(dq_ref[...], wq[...])
    zeros = jnp.zeros((BLK, width), F32)
    dnorm = dnorm + jnp.concatenate([zeros, dq, zeros], axis=0)
    back = rms_back(st_ref[...], gains_ref[1, 0:1], dnorm.astype(BF16).astype(F32))
    part = grad + back[mid]
    part_ref[...] = part
    halo_ref[:BLK] = back[:BLK]
    halo_ref[BLK:] = back[(qb - 1) * BLK :]

    _, rows_low = fold(g1_ref[0, :, :BLK], ext, ext_t, 2, 1)
    _, rows_high = fold(g1_ref[nb - 1, :, 2 * BLK :], ext, ext_t, nb + 1, nb + 2)
    pad = jnp.zeros((8, width - LANES), F32)

    def payload(halo, edge, rows):
        tail = jnp.concatenate([three_rows(rows), pad], axis=1)
        return halo, edge, jnp.concatenate([tail, jnp.zeros_like(tail)], axis=0)

    low = payload(back[:BLK], part[:BLK], rows_low)
    high = payload(back[(qb - 1) * BLK :], part[(nb - 1) * BLK :], rows_high)
    at = 0
    for x, y in zip(high, low):
        rows = slice(at, at + x.shape[0])
        paya_ref[rows] = jnp.where(even, x, y).astype(BF16)
        payb_ref[rows] = jnp.where(even, y, x).astype(BF16)
        at += x.shape[0]


def slope_kernel(_, pre_ref, out_ref):
    out_ref[...] = gelu_slope(pre_ref[...]).astype(BF16)


def last_kernel(
    nb, heads, hdim,
    par_ref, gam_ref, energy_ref, ext_ref, gains_ref, paya_ref, payb_ref, part_ref, halo_ref, g1_ref,
    o_ref, rl_ref, v_ref, x1_ref, gd_ref, e_ref, wo, wu, wd,
    f_ref,
    datt_ref, sum_ref, ends_ref,
):
    qb = nb + 2
    ext = ext_ref[...]
    ext_t = ext.T

    even = par_ref[0:1, 0:1] < 0.5
    from_a, from_b = paya_ref[...].astype(F32), payb_ref[...].astype(F32)
    from_low, from_high = arrange(even, from_a, from_b)
    part = part_ref[...]
    pieces = [halo_ref[:BLK] + from_low[BLK : 2 * BLK]]
    own_parts = [part[i * BLK : (i + 1) * BLK] for i in range(nb)]
    own_parts[0] = own_parts[0] + from_low[:BLK]
    own_parts[-1] = own_parts[-1] + from_high[:BLK]
    pieces += own_parts
    pieces.append(halo_ref[BLK:] + from_high[BLK : 2 * BLK])
    grad = jnp.concatenate(pieces, axis=0)
    du = mm_nt(grad.astype(BF16), wd[...]).astype(BF16).astype(F32)
    dinner = mm_nt((du * gd_ref[...].astype(F32)).astype(BF16), wu[...]).astype(BF16).astype(F32)
    grad = grad + rms_back(x1_ref[...], gains_ref[0, 1:2], dinner)
    datt_ref[...] = mm_nt(grad.astype(BF16), wo[...]).astype(BF16).astype(F32)

    per = LANES // hdim
    groups = heads // per
    masks = head_masks(BLK, per, hdim)
    masks2 = head_masks(2 * BLK, per, hdim)

    def cotangents(rows, g):
        cols = group_at(g)
        lane = lax.broadcasted_iota(jnp.int32, (1, LANES), 1) // hdim
        gam = jnp.zeros((1, LANES), F32)
        for h in range(per):
            gam = jnp.where(lane == h, gam_ref[0, g * per + h, 0:1], gam)
        d_o = datt_ref[rows, cols] * rl_ref[rows, cols] * gam
        return d_o.astype(BF16), delta_of(d_o * o_ref[rows, cols].astype(F32), per, hdim)

    last = qb - 1
    sum_ref[...] = g1_ref[...]
    ends_ref[...] = jnp.zeros_like(ends_ref)

    def body(i, g):
        d_o, delta = cotangents(blocks_at(i + 1, 2), g)
        prods, _ = pair_products(d_o, v_ref[blocks_at(i + 1, 4), group_at(g)], masks2, per)
        for t in range(2):
            at = slice(t * BLK, (t + 1) * BLK)
            for n, c in enumerate(window_parts(t)):
                total = sum_ref[i + t, :, c]
                for h in range(per):
                    total = total + e_ref[i + t + 1, g * per + h, :, c].astype(F32) * (prods[t][h][n] - delta[h][at])
                sum_ref[i + t, :, c] = total

    def ends(_, g):
        cols = group_at(g)
        low_o, low_delta = cotangents(slice(0, BLK), g)
        high_o, high_delta = cotangents(slice(last * BLK, qb * BLK), g)
        both = jnp.concatenate([low_o, high_o], axis=1)
        both = jnp.concatenate([both * jnp.concatenate([m, m], axis=1) for m in masks], axis=0)
        prods = mm_nt(both, beside(v_ref[2 * BLK : 3 * BLK, cols], v_ref[last * BLK : qb * BLK, cols]))
        low_sum, high_sum = ends_ref[0], ends_ref[1]
        for h in range(per):
            low = prods[h * BLK : (h + 1) * BLK, :BLK] - low_delta[h]
            high = prods[h * BLK : (h + 1) * BLK, BLK:] - high_delta[h]
            low_sum = low_sum + e_ref[0, g * per + h, :, 2 * BLK :].astype(F32) * low
            high_sum = high_sum + e_ref[last, g * per + h, :, :BLK].astype(F32) * high
        ends_ref[0] = low_sum
        ends_ref[1] = high_sum

    over(nb // 2, groups, body)
    over(1, groups, ends)
    forces = [jnp.zeros((8, LANES), F32) for _ in range(nb)]
    forces[0] = forces[0] + from_low[2 * BLK : 2 * BLK + 8, :LANES]
    forces[-1] = forces[-1] + from_high[2 * BLK : 2 * BLK + 8, :LANES]
    for i in range(nb):
        total = sum_ref[i]
        sums = None
        for s in range(3):
            cols, rows = fold(total[:, s * BLK : (s + 1) * BLK], ext, ext_t, i + 2, i + 1 + s)
            sums = cols if sums is None else [a + b for a, b in zip(sums, cols)]
            j = i - 1 + s
            if 0 <= j < nb:
                forces[j] = forces[j] + three_rows(rows)
        forces[i] = forces[i] + columns_to_rows(sums)
    _, rows = fold(ends_ref[0], ext, ext_t, 1, 2)
    forces[0] = forces[0] + three_rows(rows)
    _, rows = fold(ends_ref[1], ext, ext_t, nb + 2, nb + 1)
    forces[-1] = forces[-1] + three_rows(rows)
    f_ref[...] = jnp.concatenate(forces, axis=1)[:3]


def swap_a(x):
    n = lax.axis_size("chain")
    return lax.ppermute(x, "chain", [(i, i ^ 1) for i in range(n)])


def swap_b(x):
    n = lax.axis_size("chain")
    return lax.ppermute(x, "chain", [(i, ((i + 1) ^ 1) - 1) for i in range(1, n - 1)])


def hop(x, step):
    return lax.ppermute(x, "chain", [(i, i ^ step) for i in range(lax.axis_size("chain"))])


def local(
    species, positions, block_list, embed, w_query, w_key, w_value, w_out, w_up, w_down, norm_gains, gammas, out_gain, readout
):
    atoms = species.shape[0]
    nb = atoms // BLK
    width = embed.shape[1]
    layers, heads = gammas.shape
    hdim = width // heads
    ff = w_up.shape[2]
    qb, kb = nb + 2, nb + 4
    count = lax.axis_size("chain")
    assert nb >= 2 and layers == 2 and LANES % hdim == 0 and nb % 2 == 0 and count >= 8 and count & (count - 1) == 0
    me = lax.axis_index("chain").astype(jnp.int32)
    vm = pltpu.VMEM
    smem = pl.BlockSpec(memory_space=pltpu.SMEM)

    def work(products):
        return pl.CostEstimate(flops=products * atoms * width * width * 8, transcendentals=0, bytes_accessed=0)

    vmem = pl.BlockSpec(memory_space=vm)
    keep = functools.partial(pltpu.with_memory_space_constraint, memory_space=vm)
    pin = functools.partial(pltpu.with_memory_space_constraint, memory_space=pltpu.HBM)
    own, side = pl.pallas_call(
        functools.partial(pack_kernel, nb),
        out_shape=[vm((8, atoms), F32), vm((8, LANES), F32)],
        in_specs=[smem, smem, vmem, vmem],
        out_specs=[vmem, vmem],
    )(me.reshape(1), block_list, positions, species.reshape(1, atoms))
    edge = 2 * BLK
    if atoms == edge:
        send_a = send_b = own
    else:
        first, last = own[:, :edge], own[:, -edge:]
        send_a = jnp.where(me % 2 == 0, last, first)
        send_b = jnp.where(me % 2 == 0, first, last)
    near_a, near_b = swap_a(send_a), swap_b(send_b)
    hbm = pl.BlockSpec(memory_space=pltpu.HBM)
    table = vm(embed.shape, BF16)
    square = vm((width, width), BF16)
    small = pl.pallas_call(
        table_kernel,
        out_shape=[
            table, table, table, table, vm(norm_gains.shape, F32), vm((8, width), F32),
            vm((layers, heads, 8, LANES), F32),
        ],
        in_specs=[hbm] * 8,
        out_specs=[vmem] * 7,
        scratch_shapes=[
            square, square, square, vm((layers, heads), F32), vm((1, width), F32), vm((1, width), F32),
            pltpu.SemaphoreType.DMA((8,)),
        ],
        compiler_params=pltpu.CompilerParams(vmem_limit_bytes=8 * 1024 * 1024),
        cost_estimate=work(1),
    )(
        pin(w_query), pin(embed), pin(norm_gains), pin(w_key), pin(w_value), pin(gammas),
        pin(out_gain.reshape(1, width)), pin(readout.reshape(1, width)),
    )
    *tables, gains, w, rates = (keep(x) for x in small)
    side = keep(side)
    weights = (w_query, w_key, w_value, w_out, w_up, w_down)
    shapes = [vm((width, width), BF16)] * 4 + [vm((width, ff), BF16), vm((ff, width), BF16)]
    first = pl.pallas_call(
        functools.partial(first_kernel, nb, heads, hdim),
        out_shape=[
            vm((8, LANES), F32), vm((8, kb * BLK), F32),
            vm((qb * BLK, width), BF16), vm((qb * BLK, width), F32), vm((kb * BLK, width), BF16),
            vm((qb * BLK, width), F32), vm((qb * BLK, ff), F32), vm((qb, heads, BLK, 3 * BLK), BF16), *shapes[3:],
            vm((qb * BLK, width), F32), vm((nb * BLK, width), BF16), vm((qb * BLK, width), BF16),
            vm((qb * BLK, width), BF16), vm((nb * BLK, width), BF16), vm((nb * BLK, width), F32),
            vm((nb, heads, BLK, 3 * BLK), BF16), vm((nb * BLK, width), F32), vm((nb * BLK, ff), F32),
            vm((nb * BLK, width), F32), *shapes,
        ],
        in_specs=[vmem] * 11 + [hbm] * 6,
        out_specs=[vmem] * 27,
        scratch_shapes=[
            vm((qb, BLK, 3 * BLK), F32), vm((qb * BLK, width), F32), vm((qb * BLK, width), BF16),
            vm((kb * BLK, width), BF16), vm((LANES // hdim, kb * BLK, width), BF16),
            vm((LANES // hdim, qb * BLK, width), BF16), pltpu.SemaphoreType.DMA((2, 6)),
        ],
        compiler_params=pltpu.CompilerParams(vmem_limit_bytes=20 * 1024 * 1024),
        cost_estimate=work(qb * 7),
    )(
        side, rates, keep(own), keep(near_a), keep(near_b), *tables, gains, w, *(pin(x) for x in weights),
    )
    energy, ext = first[0], keep(first[1])
    saved0 = [keep(x) for x in first[2:11]]
    saved1 = [keep(x) for x in first[11:]]
    energy = energy + hop(energy, 1)
    pay = vm((2 * BLK + 16, width), BF16)
    (st, q1, k1, v1, o1, rl1, e1, x11, gd1, top), (wq1, wk1, wv1, wo1, wu1, wd1) = saved1[:10], saved1[10:]
    own_rows = vm((nb * BLK, width), F32)
    grad, datt = pl.pallas_call(
        feed_back_kernel,
        out_shape=[own_rows, own_rows],
        in_specs=[vmem] * 7,
        out_specs=[vmem] * 2,
        compiler_params=pltpu.CompilerParams(vmem_limit_bytes=12 * 1024 * 1024),
        cost_estimate=work(nb * 3),
    )(gains, x11, gd1, top, wo1, wu1, wd1)
    pay_a, pay_b, part, halo, pairs = pl.pallas_call(
        functools.partial(middle_kernel, nb, heads, hdim),
        out_shape=[pay, pay, vm((nb * BLK, width), F32), vm((2 * BLK, width), F32), vm((nb, BLK, 3 * BLK), F32)],
        in_specs=[vmem] * 17,
        out_specs=[vmem] * 5,
        scratch_shapes=[
            vm((nb * BLK, width), BF16), vm((width, qb * BLK), F32), vm((width, qb * BLK), F32),
        ],
        compiler_params=pltpu.CompilerParams(vmem_limit_bytes=20 * 1024 * 1024),
        cost_estimate=work(nb * 9),
    )(
        side, rates, keep(energy), ext, gains, st, q1, k1, v1, o1, rl1, e1, keep(grad), keep(datt), wq1, wk1, wv1
    )
    energy = energy + hop(energy, 2)
    energy, pay_a, pay_b = lax.optimization_barrier((energy, pay_a, pay_b))
    saved0[4] = keep(
        pl.pallas_call(
            slope_kernel,
            out_shape=vm((qb * BLK, ff), BF16),
            in_specs=[vmem, vmem],
            out_specs=vmem,
            compiler_params=pltpu.CompilerParams(vmem_limit_bytes=8 * 1024 * 1024),
            cost_estimate=work(qb),
        )(keep(energy), saved0[4])
    )
    arriving = hop(energy, 4)
    got_a, got_b = swap_a(pay_a), swap_b(pay_b)
    energy = energy + arriving
    forces = pl.pallas_call(
        functools.partial(last_kernel, nb, heads, hdim),
        out_shape=jax.ShapeDtypeStruct((3, atoms), F32),
        in_specs=[vmem] * 19,
        out_specs=vmem,
        scratch_shapes=[vm((qb * BLK, width), F32), vm((nb, BLK, 3 * BLK), F32), vm((2, BLK, BLK), F32)],
        compiler_params=pltpu.CompilerParams(vmem_limit_bytes=20 * 1024 * 1024),
        cost_estimate=work(qb * 3),
    )(
        side, rates, keep(energy), ext, gains, keep(got_a), keep(got_b), keep(part), keep(halo), keep(pairs), *saved0
    )
    if count > 8:
        arriving = hop(energy, 8)
        energy, forces = lax.optimization_barrier((energy, forces))
        energy = energy + arriving
    step = 16
    while step < count:
        energy = energy + hop(energy, step)
        step *= 2
    return energy[:1, :1].reshape(1), forces


def solution(mesh):
    sharded = ("frames", "chain")
    return jax.shard_map(
        local,
        mesh=mesh,
        in_specs=(P(sharded), P(None, sharded), P(sharded, None)) + (P(),) * 11,
        out_specs=(P("frames"), P(None, sharded)),
        check_vma=False,
    )
```
